512 devices in a mesh: batch: 32 (over y, x, core), seq: 16 (over z).
Axes of the slice: x: 4, y: 4, z: 16, core: 2. Of those that a mesh axis runs over, the one named last changes fastest.
Arguments:
- events: bfloat16 [131072, 256], P(('batch', 'seq')), parts along dimension 0, may hold values from -6 to 6
- positions: int32 [131072], P(('batch', 'seq')), parts along dimension 0, may hold values from 0 to 4095, as said below
- length: int32 [32], P('batch'), parts along dimension 0, may hold values from 2048 to 4096
- filters: float32 [4096, 2, 256], P('seq'), may hold values from -0.09375 to 0.09375
- skip_gain: float32 [2, 256], replicated, may hold values from 0.5 to 1.5
- short_filter: float32 [3, 768], replicated, may hold values from -3 to 3
- in_proj: bfloat16 [256, 768], replicated, may hold values from -0.375 to 0.375
- out_proj: bfloat16 [256, 256], replicated, may hold values from -0.375 to 0.375
Outputs:
- layer_out: bfloat16 [131072, 256], P(('batch', 'seq')), parts along dimension 0
The draws below stay inside these ranges and needn't reach their ends.
There are 32 independent parts, one for each index of `batch`. The reference program is written for one: setup_inputs(seed, part) draws one part's arguments, and reference() takes and returns one part's arrays. A program takes and returns all parts, laid end to end along the dimension named above; an argument that names none is the same for every part. Nothing has to cross between parts.
Inputs may be any that keep to these rules, and one draw needn't show every extreme that they name: positions is a permutation of 0 to 4095. Cut each row block b (positions b * 256 to (b + 1) * 256 - 1) into runs of 16 positions, run c starting at b * 256 + c * 16. The rows of one seq device hold whole runs only, exactly one run of each row block and exactly one run of each index c, in any order.
All inputs are finite; a program needn't handle non-finite values.
Results may differ from the reference program's by a relative error of at most 0.007.
Values may be sent and summed in bfloat16 or wider, within the bound.
A program may use at most 64 MiB of HBM per device.

```python
import jax
import jax.numpy as jnp

D = 256
TOK_DEV = 256
TOKENS = 4096
N_SEQ = 16


def draw_positions(key, part):
    key_rows, key_cols, key_order = jax.random.split(key, 3)
    col_size = TOK_DEV // N_SEQ
    row_shift = jax.random.permutation(key_rows, N_SEQ)
    col_shift = jax.random.permutation(key_cols, N_SEQ)
    col_inverse = jnp.argsort(col_shift)
    source_ids = jnp.arange(N_SEQ, dtype=jnp.int32)[:, None]
    block_ids = jnp.arange(N_SEQ, dtype=jnp.int32)[None, :]
    column_ids = col_inverse[(source_ids - row_shift[block_ids]) % N_SEQ]
    starts = block_ids * TOK_DEV + column_ids * col_size
    offsets = jnp.arange(col_size, dtype=jnp.int32)[None, None, :]
    placed = (starts[:, :, None] + offsets).reshape(N_SEQ, TOK_DEV)
    row_keys = jax.random.split(key_order, N_SEQ)
    shuffles = jax.vmap(lambda one_key: jax.random.permutation(one_key, TOK_DEV))(row_keys)
    placed = jnp.take_along_axis(placed, shuffles, axis=1)
    return placed.reshape(-1).astype(jnp.int32)


def block_levels(own_key, shape, cuts, least, largest):
    level = 1.0
    for position, blocks in cuts:
        heights = jax.random.uniform(jax.random.fold_in(jax.random.fold_in(own_key, 6), position), (blocks,), jnp.float32, least / len(cuts), largest / len(cuts))
        level = level * jnp.repeat(jnp.exp(heights), shape[position] // blocks).reshape((-1,) + (1,) * (len(shape) - 1 - position))
    return level


def centred(rng, shape, spread, most, cuts=(), held_as=jnp.bfloat16):
    entries = jax.random.normal(rng, shape, jnp.float32) * spread
    if len(cuts) > 0:
        entries = block_levels(rng, shape, cuts, -0.22, 0.18) * entries
    return jnp.clip(entries, min=-most, max=most).astype(held_as)


def setup_inputs(seed: int = 0, part: int = 0) -> dict:
    key_list = jax.random.split(jax.random.key(seed), 9)
    part_keys = jax.random.split(jax.random.fold_in(key_list[8], part), 9)
    return {
        "events": centred(part_keys[0], (TOKENS, D), 1.0, 6.0, ((0, 16),)),
        "positions": draw_positions(jax.random.fold_in(jax.random.fold_in(key_list[8], part), 71), part),
        "length": jax.random.randint(part_keys[2], (1,), TOKENS // 2, TOKENS + 1).astype(jnp.int32),
        "filters": centred(key_list[3], (TOKENS, 2, D), TOKENS ** -0.5, 0.09375, ((0, 16),), jnp.float32),
        "skip_gain": jnp.clip(jax.random.uniform(key_list[4], (2, D), jnp.float32, 0.5, 1.5), 0.5, 1.5),
        "short_filter": centred(key_list[5], (3, 3 * D), 0.6, 3.0, (), jnp.float32),
        "in_proj": centred(key_list[6], (D, 3 * D), D ** -0.5, 0.375),
        "out_proj": centred(key_list[7], (D, D), D ** -0.5, 0.375),
    }


def long_conv(signal, taps):
    padded_len = 2 * signal.shape[0]
    spectrum = jnp.fft.rfft(signal, n=padded_len, axis=0) * jnp.fft.rfft(taps, n=padded_len, axis=0)
    return jnp.fft.irfft(spectrum, n=padded_len, axis=0)[:signal.shape[0]].astype(jnp.float32)


def reference(events, positions, length, filters, skip_gain, short_filter, in_proj, out_proj):
    stream = jnp.zeros_like(events).at[positions].set(events)
    keep_rows = (jnp.arange(TOKENS, dtype=jnp.int32) < length[0])[:, None]
    stream = jnp.where(keep_rows, stream, jnp.zeros_like(stream))
    projected = jnp.dot(stream, in_proj, preferred_element_type=jnp.float32).astype(jnp.bfloat16)
    widened = projected.astype(jnp.float32)
    padded = jnp.pad(widened, ((2, 0), (0, 0)))
    shorted = short_filter[0] * widened + short_filter[1] * padded[1:-1] + short_filter[2] * padded[:-2]
    value = shorted[:, :D]
    gate_one = shorted[:, D:2 * D]
    gate_two = shorted[:, 2 * D:]
    first = gate_one * (long_conv(value, filters[:, 0]) + skip_gain[0] * value)
    second = long_conv(first, filters[:, 1]) + skip_gain[1] * first
    gated = (gate_two * second).astype(jnp.bfloat16)
    return jnp.dot(gated, out_proj, preferred_element_type=jnp.float32).astype(jnp.bfloat16)
```

```python
import functools
import math

import jax
import jax.numpy as jnp
import ml_dtypes
import numpy as np
from jax import lax
from jax.experimental import pallas as pl
from jax.experimental.pallas import tpu as pltpu
from jax.sharding import PartitionSpec as P

N = 16
W = 256
POINTS = 2 * N * W
F32, BF16 = jnp.float32, jnp.bfloat16


def split(table):
    high = table.astype(ml_dtypes.bfloat16)
    low = (table - high.astype(np.float64)).astype(ml_dtypes.bfloat16)
    return high, low


@functools.cache
def make_tables():
    half = np.arange(N) + 0.5
    outer = 2 * np.pi * np.outer(half, np.arange(N)) / (2 * N)
    eye = np.eye(N)
    fwd_a = np.concatenate([np.kron(np.cos(outer), eye), np.kron(-np.sin(outer), eye)], 0)
    inv_a = np.concatenate([np.kron(np.cos(outer.T), eye), np.kron(-np.sin(outer.T), eye)], 1) * (2.0 / POINTS)
    inner = 2 * np.pi * (np.outer(np.arange(W), np.arange(W)) % W) / W
    cos, sin = np.cos(inner), np.sin(inner)
    fwd_b = np.block([[cos, -sin], [sin, cos]])
    inv_b = np.block([[cos, sin], [-sin, cos]])
    twist = 2 * np.pi * np.outer(half, np.arange(W)) / POINTS
    cat = lambda table, axis: np.concatenate([split(table)[i] for i in (0, 0, 1)], axis)
    return (
        cat(fwd_a, 1),
        cat(fwd_b, 0),
        cat(inv_b, 0),
        cat(inv_a, 1),
        np.stack([np.cos(twist), np.sin(twist)]).astype(np.float32),
    )


def parts(x, axis):
    high = x.astype(BF16)
    low = (x - high.astype(F32)).astype(BF16)
    return jnp.concatenate([high, low, high], axis=axis)


def dot(a, b, dims=((1,), (0,))):
    return lax.dot_general(a, b, (dims, ((), ())), preferred_element_type=F32)


def kernel(
    n_batch,
    length,
    positions,
    events,
    filters,
    skip_gain,
    short_filter,
    in_proj,
    out_proj,
    fwd_a_hbm,
    fwd_b_hbm,
    inv_b_hbm,
    inv_a_hbm,
    twist_hbm,
    out,
    fwd_a,
    fwd_b,
    inv_b,
    inv_a,
    twist,
    thirds,
    block_row,
    taps,
    gated,
    recv_sig,
    recv_blk,
    recv_tap,
    recv_out,
    spec,
    table_sem,
    sig_send,
    sig_recv,
    blk_send,
    blk_recv,
    tap_send,
    tap_recv,
    own_send,
    own_recv,
    out_send,
    out_recv,
):
    me = lax.axis_index("seq")
    lane = lax.axis_index("batch")
    column, core = lane // 2, lane % 2

    barrier = pltpu.get_barrier_semaphore()

    def greet(k, carry):
        pl.semaphore_signal(barrier, inc=1, device_id={"seq": (me + k) % N})
        return carry

    def greet_plane(k, carry):
        pl.semaphore_signal(barrier, inc=1, device_id={"batch": (lane + k) % n_batch})
        return carry

    lax.fori_loop(1, N, greet, 0)
    lax.fori_loop(1, n_batch, greet_plane, 0)

    tables = [
        pltpu.make_async_copy(src, dst, table_sem.at[i])
        for i, (src, dst) in enumerate(
            ((fwd_a_hbm, fwd_a), (twist_hbm, twist), (fwd_b_hbm, fwd_b), (inv_b_hbm, inv_b), (inv_a_hbm, inv_a))
        )
    ]
    for copy in tables:
        copy.start()

    target = (me + column) % N
    rows16 = lax.broadcasted_iota(jnp.int32, (N, W), 0)
    lanes16 = lax.broadcasted_iota(jnp.int32, (N, W), 1)
    pick = (lanes16 == rows16 + target * N).astype(BF16)
    lags = jnp.where(core == 0, filters[:, 0:W], filters[:, W : 2 * W]).astype(BF16)
    taps[...] = dot(pick, lags, ((1,), (1,))).astype(BF16)

    pos = positions[...]
    order = lax.broadcasted_iota(jnp.int32, (W, W), 0) == pos % W
    one_hot = order.astype(BF16)
    kept = jnp.where(pos < length[0], one_hot, jnp.zeros_like(one_hot))
    ids = jnp.broadcast_to((pos // W).astype(BF16), (N, W))
    block_row[...] = dot(ids, one_hot, ((1,), (1,)))[0:8].astype(jnp.int32)
    ordered = dot(kept, events[...]).astype(BF16)
    for t in range(3):
        projected = dot(ordered, in_proj[:, t * W : (t + 1) * W])
        thirds[t] = projected.T.astype(BF16).reshape(N, N, W)

    pl.semaphore_wait(barrier, N - 1 + n_batch - 1)

    def tap_first():
        return pltpu.make_async_remote_copy(
            src_ref=taps,
            dst_ref=recv_tap.at[core, me],
            send_sem=own_send,
            recv_sem=own_recv,
            device_id={"seq": target},
        )

    slot = (me + N - column) % N

    @pl.when(column != 0)
    def _():
        tap_first().start()

    @pl.when(column == 0)
    def _():
        recv_tap[core, me] = taps[...]

    def block_copy(k):
        peer = (me + k) % N
        return pltpu.make_async_remote_copy(
            src_ref=block_row,
            dst_ref=recv_blk.at[me],
            send_sem=blk_send.at[peer],
            recv_sem=blk_recv.at[me],
            device_id={"seq": peer},
        )

    def block_arrival(k):
        peer = (me + k) % N
        return pltpu.make_async_remote_copy(
            src_ref=block_row,
            dst_ref=recv_blk.at[peer],
            send_sem=blk_send.at[peer],
            recv_sem=blk_recv.at[peer],
            device_id={"seq": peer},
        )

    def third_copy(t, k):
        peer = (me + k) % N
        return pltpu.make_async_remote_copy(
            src_ref=thirds.at[t, peer],
            dst_ref=recv_sig.at[t, me],
            send_sem=sig_send.at[t, peer],
            recv_sem=sig_recv.at[t, me],
            device_id={"seq": peer},
        )

    def third_arrival(t, k):
        peer = (me + k) % N
        return pltpu.make_async_remote_copy(
            src_ref=thirds.at[t, peer],
            dst_ref=recv_sig.at[t, peer],
            send_sem=sig_send.at[t, peer],
            recv_sem=sig_recv.at[t, peer],
            device_id={"seq": peer},
        )

    def each(count, act):
        def step(k, carry):
            act(k)
            return carry

        lax.fori_loop(1, count, step, 0)

    each(N, lambda k: block_copy(k).start())
    for t in range(3):
        each(N, lambda k: third_copy(t, k).start())
    recv_blk[me] = block_row[...]
    for t in range(3):
        recv_sig[t, me] = thirds[t, me]

    @pl.when(column != 0)
    def _():
        pltpu.make_async_remote_copy(
            src_ref=taps,
            dst_ref=recv_tap.at[core, slot],
            send_sem=own_send,
            recv_sem=own_recv,
            device_id={"seq": target},
        ).wait_recv()

    def tap_copy(k):
        peer = (lane + k) % n_batch
        return pltpu.make_async_remote_copy(
            src_ref=recv_tap.at[core, slot],
            dst_ref=recv_tap.at[core, slot],
            send_sem=tap_send.at[peer],
            recv_sem=tap_recv.at[lane],
            device_id={"batch": peer},
        )

    def tap_arrival(k):
        peer = (lane + k) % n_batch
        there = recv_tap.at[peer % 2, (me + N - peer // 2) % N]
        return pltpu.make_async_remote_copy(
            src_ref=there,
            dst_ref=there,
            send_sem=tap_send.at[peer],
            recv_sem=tap_recv.at[peer],
            device_id={"batch": peer},
        )

    each(n_batch, lambda k: tap_copy(k).start())

    def column_of(row):
        return jnp.sum(jnp.where(lanes16 == rows16 + me * N, row, 0.0), axis=1, keepdims=True)[None]

    def rotate(re, im, sign):
        cos = twist[0][:, None, :]
        sin = twist[1][:, None, :] * sign
        re, im = re.reshape(N, N, W), im.reshape(N, N, W)
        return (re * cos + im * sin).reshape(W, W), (im * cos - re * sin).reshape(W, W)

    def forward(signal):
        mid = dot(fwd_a[...], parts(signal, 0))
        re, im = rotate(mid[:W], mid[W:], 1.0)
        return dot(parts(jnp.concatenate([re, im], axis=1), 1), fwd_b[...])

    def inverse(re, im):
        mid = dot(parts(jnp.concatenate([re, im], axis=1), 1), inv_b[...])
        re, im = rotate(mid[:, :W], mid[:, W:], -1.0)
        return dot(inv_a[...], parts(jnp.concatenate([re, im], axis=0), 0))

    def convolve(signal, f):
        got = forward(signal)
        re, im = got[:, :W], got[:, W:]
        tap_re, tap_im = spec[f, :, :W], spec[f, :, W:]
        return inverse(re * tap_re - im * tap_im, re * tap_im + im * tap_re)

    sub = lax.broadcasted_iota(jnp.int32, (W, W), 1)

    def short(t):
        rows = []
        got = [recv_sig[t, s].astype(F32) for s in range(N)]
        for b in range(N):
            total = jnp.zeros((N, W), F32)
            for s in range(N):
                row = jnp.concatenate([recv_blk[s, 0:1, :]], axis=0)
                total = jnp.where(row == b, got[s], total)
            rows.append(total)
        stream = jnp.concatenate(rows, axis=0)
        before = jnp.concatenate([jnp.zeros((N, W), F32), stream[:-N]], axis=0)
        one = pltpu.roll(jnp.where(sub == W - 1, before, stream), 1, 1)
        two = pltpu.roll(jnp.where(sub >= W - 2, before, stream), 2, 1)
        tap = [column_of(short_filter[i : i + 1, t * W : (t + 1) * W]) for i in range(3)]
        blocks = lambda x: x.reshape(N, N, W)
        return (tap[0] * blocks(stream) + tap[1] * blocks(one) + tap[2] * blocks(two)).reshape(W, W)

    for copy in tables:
        copy.wait()
    each(N, lambda k: block_arrival(k).wait_recv())
    each(n_batch, lambda k: tap_arrival(k).wait_recv())
    for f in range(2):
        spec[f] = forward(recv_tap[f].reshape(W, W).astype(F32))

    each(N, lambda k: third_arrival(0, k).wait_recv())
    value = short(0)
    gain = [column_of(skip_gain[i : i + 1, :]) for i in range(2)]
    scaled = lambda g, x: (g * x.reshape(N, N, W)).reshape(W, W)
    first = convolve(value, 0) + scaled(gain[0], value)
    each(N, lambda k: third_arrival(1, k).wait_recv())
    first = short(1) * first
    second = convolve(first, 1) + scaled(gain[1], first)
    each(N, lambda k: third_arrival(2, k).wait_recv())
    gated[...] = (short(2) * second).astype(BF16).reshape(N, N, W)

    def out_copy(k):
        peer = (me + k) % N
        return pltpu.make_async_remote_copy(
            src_ref=gated.at[peer],
            dst_ref=recv_out.at[me],
            send_sem=out_send.at[peer],
            recv_sem=out_recv.at[me],
            device_id={"seq": peer},
        )

    def out_arrival(k):
        peer = (me + k) % N
        return pltpu.make_async_remote_copy(
            src_ref=gated.at[peer],
            dst_ref=recv_out.at[peer],
            send_sem=out_send.at[peer],
            recv_sem=out_recv.at[peer],
            device_id={"seq": peer},
        )

    each(N, lambda k: out_copy(k).start())
    recv_out[me] = gated[me]

    @pl.when(column != 0)
    def _():
        tap_first().wait_send()

    each(N, lambda k: block_copy(k).wait_send())
    for t in range(3):
        each(N, lambda k: third_copy(t, k).wait_send())
    each(n_batch, lambda k: tap_copy(k).wait_send())
    each(N, lambda k: out_copy(k).wait_send())
    each(N, lambda k: out_arrival(k).wait_recv())
    whole = recv_out[...].reshape(W, W)
    out[...] = dot(whole, out_proj[...], ((0,), (0,))).astype(BF16)


def body(n_batch, events, positions, length, filters, skip_gain, short_filter, in_proj, out_proj):
    tables = [jnp.asarray(table) for table in make_tables()]
    vmem, smem, anywhere = (pl.BlockSpec(memory_space=m) for m in (pltpu.VMEM, pltpu.SMEM, pl.ANY))
    dma = lambda *shape: pltpu.SemaphoreType.DMA(shape)
    return pl.pallas_call(
        functools.partial(kernel, n_batch),
        out_shape=jax.ShapeDtypeStruct((W, W), BF16),
        in_specs=[smem] + [vmem] * 7 + [anywhere] * 5,
        out_specs=vmem,
        scratch_shapes=[pltpu.VMEM(table.shape, table.dtype) for table in tables]
        + [
            pltpu.VMEM((3, N, N, W), BF16),
            pltpu.VMEM((8, W), jnp.int32),
            pltpu.VMEM((N, W), BF16),
            pltpu.VMEM((N, N, W), BF16),
            pltpu.VMEM((3, N, N, W), BF16),
            pltpu.VMEM((N, 8, W), jnp.int32),
            pltpu.VMEM((2, N, N, W), BF16),
            pltpu.VMEM((N, N, W), BF16),
            pltpu.VMEM((2, W, 2 * W), F32),
            dma(5),
            dma(3, N),
            dma(3, N),
            dma(N),
            dma(N),
            dma(n_batch),
            dma(n_batch),
            pltpu.SemaphoreType.DMA,
            pltpu.SemaphoreType.DMA,
            dma(N),
            dma(N),
        ],
        compiler_params=pltpu.CompilerParams(
            collective_id=0, has_side_effects=True, vmem_limit_bytes=48 * 1024 * 1024
        ),
    )(
        length,
        positions.reshape(1, W),
        events,
        filters.reshape(W, 2 * W),
        skip_gain,
        short_filter,
        in_proj,
        out_proj,
        *tables,
    )


def solution(mesh):
    return jax.shard_map(
        functools.partial(body, mesh.shape["batch"]),
        mesh=mesh,
        in_specs=(
            P(("batch", "seq"), None),
            P(("batch", "seq")),
            P("batch"),
            P("seq", None, None),
            P(),
            P(),
            P(),
            P(),
        ),
        out_specs=P(("batch", "seq"), None),
        check_vma=False,
    )
```

```python
import functools
import math

import jax
import jax.numpy as jnp
import ml_dtypes
import numpy as np
from jax import lax
from jax.experimental import pallas as pl
from jax.experimental.pallas import tpu as pltpu
from jax.sharding import PartitionSpec as P

N = 16
W = 256
POINTS = 2 * N * W
F32, BF16 = jnp.float32, jnp.bfloat16


def split(table):
    high = table.astype(ml_dtypes.bfloat16)
    low = (table - high.astype(np.float64)).astype(ml_dtypes.bfloat16)
    return high, low


@functools.cache
def make_tables():
    half = np.arange(N) + 0.5
    outer = 2 * np.pi * np.outer(half, np.arange(N)) / (2 * N)
    eye = np.eye(N)
    fwd_a = np.concatenate([np.kron(np.cos(outer), eye), np.kron(-np.sin(outer), eye)], 0)
    inv_a = np.concatenate([np.kron(np.cos(outer.T), eye), np.kron(-np.sin(outer.T), eye)], 1) * (2.0 / POINTS)
    inner = 2 * np.pi * (np.outer(np.arange(W), np.arange(W)) % W) / W
    cos, sin = np.cos(inner), np.sin(inner)
    fwd_b = np.block([[cos, -sin], [sin, cos]])
    inv_b = np.block([[cos, sin], [-sin, cos]])
    twist = 2 * np.pi * np.outer(half, np.arange(W)) / POINTS
    cat = lambda table, axis: np.concatenate([split(table)[i] for i in (0, 0, 1)], axis)
    return (
        cat(fwd_a, 1),
        cat(fwd_b, 0),
        cat(inv_b, 0),
        cat(inv_a, 1),
        np.stack([np.cos(twist), np.sin(twist)]).astype(np.float32),
    )


def parts(x, axis):
    high = x.astype(BF16)
    low = (x - high.astype(F32)).astype(BF16)
    return jnp.concatenate([high, low, high], axis=axis)


def dot(a, b, dims=((1,), (0,))):
    return lax.dot_general(a, b, (dims, ((), ())), preferred_element_type=F32)


INPUTS = 13


def kernel(n_batch, *refs):
    outside, (out, *inside), rest = refs[:INPUTS], refs[INPUTS : 2 * INPUTS + 1], refs[2 * INPUTS + 1 :]
    length, positions, events, filters, skip_gain, short_filter, in_proj, out_proj, *tables = inside
    fwd_a, fwd_b, inv_b, inv_a, twist = tables
    (
        thirds,
        block_row,
        taps,
        gated,
        recv_sig,
        recv_blk,
        recv_tap,
        recv_out,
        spec,
        load_sem,
        sig_send,
        sig_recv,
        blk_send,
        blk_recv,
        tap_send,
        tap_recv,
        own_send,
        own_recv,
        out_send,
        out_recv,
    ) = rest
    me = lax.axis_index("seq")
    lane = lax.axis_index("batch")
    column, core = lane // 2, lane % 2

    target = (me + column) % N
    loads = []
    for i, (src, dst) in enumerate(zip(outside, inside)):
        if i == 3:
            src = src.at[:, :, pl.ds(pl.multiple_of(target // 8 * 128, 128), 128)]
        loads.append(pltpu.make_async_copy(src, dst, load_sem.at[i]))
    for i in (1, 2, 6, 0, 3, 8, 12, 9, 5, 4, 10, 11, 7):
        loads[i].start()

    barrier = pltpu.get_barrier_semaphore()

    def greet(k, carry):
        pl.semaphore_signal(barrier, inc=1, device_id={"seq": (me + k) % N})
        return carry

    def greet_plane(k, carry):
        pl.semaphore_signal(barrier, inc=1, device_id={"batch": (lane + k) % n_batch})
        return carry

    lax.fori_loop(1, N, greet, 0)
    lax.fori_loop(1, n_batch, greet_plane, 0)

    for i in (1, 0, 2, 6):
        loads[i].wait()
    pos = positions[...]
    order = lax.broadcasted_iota(jnp.int32, (W, W), 0) == pos % W
    one_hot = order.astype(BF16)
    kept = jnp.where(pos < length[...], one_hot, jnp.zeros_like(one_hot))
    ids = jnp.broadcast_to((pos // W).astype(BF16), (N, W))
    block_row[...] = dot(ids, one_hot, ((1,), (1,)))[0:1].astype(jnp.int32)
    ordered = dot(kept, events[...]).astype(BF16)

    def project(t):
        projected = dot(ordered, in_proj[:, t * W : (t + 1) * W])
        thirds[t] = projected.T.astype(BF16).reshape(N, N, W)

    project(0)
    pl.semaphore_wait(barrier, N - 1 + n_batch - 1)

    rows16 = lax.broadcasted_iota(jnp.int32, (N, W), 0)
    lanes16 = lax.broadcasted_iota(jnp.int32, (N, W), 1)

    def tap_first():
        return pltpu.make_async_remote_copy(
            src_ref=taps,
            dst_ref=recv_tap.at[core, me],
            send_sem=own_send,
            recv_sem=own_recv,
            device_id={"seq": target},
        )

    slot = (me + N - column) % N

    def block_copy(k):
        peer = (me + k) % N
        return pltpu.make_async_remote_copy(
            src_ref=block_row,
            dst_ref=recv_blk.at[me],
            send_sem=blk_send.at[peer],
            recv_sem=blk_recv.at[me],
            device_id={"seq": peer},
        )

    def block_arrival(k):
        peer = (me + k) % N
        return pltpu.make_async_remote_copy(
            src_ref=block_row,
            dst_ref=recv_blk.at[peer],
            send_sem=blk_send.at[peer],
            recv_sem=blk_recv.at[peer],
            device_id={"seq": peer},
        )

    def third_copy(t, k):
        peer = (me + k) % N
        return pltpu.make_async_remote_copy(
            src_ref=thirds.at[t, peer],
            dst_ref=recv_sig.at[t, me],
            send_sem=sig_send.at[t, peer],
            recv_sem=sig_recv.at[t, me],
            device_id={"seq": peer},
        )

    def third_arrival(t, k):
        peer = (me + k) % N
        return pltpu.make_async_remote_copy(
            src_ref=thirds.at[t, peer],
            dst_ref=recv_sig.at[t, peer],
            send_sem=sig_send.at[t, peer],
            recv_sem=sig_recv.at[t, peer],
            device_id={"seq": peer},
        )

    def each(count, act):
        def step(k, carry):
            act(k)
            return carry

        lax.fori_loop(1, count, step, 0)

    each(N, lambda k: block_copy(k).start())
    each(N, lambda k: third_copy(0, k).start())
    recv_blk[me] = block_row[...]
    recv_sig[0, me] = thirds[0, me]

    loads[3].wait()
    pick = (lanes16[:, :128] == rows16[:, :128] + target % 8 * N).astype(BF16)
    lags = jnp.where(core == 0, filters[:, 0, :], filters[:, 1, :]).astype(BF16)
    taps[...] = dot(pick, lags, ((1,), (1,))).astype(BF16)

    @pl.when(column != 0)
    def _():
        tap_first().start()

    @pl.when(column == 0)
    def _():
        recv_tap[core, me] = taps[...]

    for t in (1, 2):
        project(t)
        each(N, lambda k: third_copy(t, k).start())
        recv_sig[t, me] = thirds[t, me]

    @pl.when(column != 0)
    def _():
        pltpu.make_async_remote_copy(
            src_ref=taps,
            dst_ref=recv_tap.at[core, slot],
            send_sem=own_send,
            recv_sem=own_recv,
            device_id={"seq": target},
        ).wait_recv()

    def tap_copy(k):
        peer = (lane + k) % n_batch
        return pltpu.make_async_remote_copy(
            src_ref=recv_tap.at[core, slot],
            dst_ref=recv_tap.at[core, slot],
            send_sem=tap_send.at[peer],
            recv_sem=tap_recv.at[lane],
            device_id={"batch": peer},
        )

    def tap_arrival(k):
        peer = (lane + k) % n_batch
        there = recv_tap.at[peer % 2, (me + N - peer // 2) % N]
        return pltpu.make_async_remote_copy(
            src_ref=there,
            dst_ref=there,
            send_sem=tap_send.at[peer],
            recv_sem=tap_recv.at[peer],
            device_id={"batch": peer},
        )

    each(n_batch, lambda k: tap_copy(k).start())

    def column_of(row):
        return jnp.sum(jnp.where(lanes16 == rows16 + me * N, row, 0.0), axis=1, keepdims=True)[None]

    def rotate(re, im, sign):
        cos = twist[0][:, None, :]
        sin = twist[1][:, None, :] * sign
        re, im = re.reshape(N, N, W), im.reshape(N, N, W)
        return (re * cos + im * sin).reshape(W, W), (im * cos - re * sin).reshape(W, W)

    def forward(signal):
        mid = dot(fwd_a[...], parts(signal, 0))
        re, im = rotate(mid[:W], mid[W:], 1.0)
        return dot(parts(jnp.concatenate([re, im], axis=1), 1), fwd_b[...])

    def inverse(re, im):
        mid = dot(parts(jnp.concatenate([re, im], axis=1), 1), inv_b[...])
        re, im = rotate(mid[:, :W], mid[:, W:], -1.0)
        return dot(inv_a[...], parts(jnp.concatenate([re, im], axis=0), 0))

    def convolve(signal, f):
        got = forward(signal)
        re, im = got[:, :W], got[:, W:]
        tap_re, tap_im = spec[f, :, :W], spec[f, :, W:]
        return inverse(re * tap_re - im * tap_im, re * tap_im + im * tap_re)

    sub = lax.broadcasted_iota(jnp.int32, (W, W), 1)

    def short(t):
        rows = []
        got = [recv_sig[t, s].astype(F32) for s in range(N)]
        for b in range(N):
            total = jnp.zeros((N, W), F32)
            for s in range(N):
                total = jnp.where(recv_blk[s] == b, got[s], total)
            rows.append(total)
        stream = jnp.concatenate(rows, axis=0)
        before = jnp.concatenate([jnp.zeros((N, W), F32), stream[:-N]], axis=0)
        one = pltpu.roll(jnp.where(sub == W - 1, before, stream), 1, 1)
        two = pltpu.roll(jnp.where(sub >= W - 2, before, stream), 2, 1)
        tap = [column_of(short_filter[i : i + 1, t * W : (t + 1) * W]) for i in range(3)]
        blocks = lambda x: x.reshape(N, N, W)
        return (tap[0] * blocks(stream) + tap[1] * blocks(one) + tap[2] * blocks(two)).reshape(W, W)

    for i in (8, 12, 9, 5, 4, 10, 11, 7):
        loads[i].wait()
    each(N, lambda k: block_arrival(k).wait_recv())
    each(n_batch, lambda k: tap_arrival(k).wait_recv())
    for f in range(2):
        spec[f] = forward(recv_tap[f].reshape(W, W).astype(F32))

    each(N, lambda k: third_arrival(0, k).wait_recv())
    value = short(0)
    gain = [column_of(skip_gain[i : i + 1, :]) for i in range(2)]
    scaled = lambda g, x: (g * x.reshape(N, N, W)).reshape(W, W)
    first = convolve(value, 0) + scaled(gain[0], value)
    each(N, lambda k: third_arrival(1, k).wait_recv())
    first = short(1) * first
    second = convolve(first, 1) + scaled(gain[1], first)
    each(N, lambda k: third_arrival(2, k).wait_recv())
    gated[...] = (short(2) * second).astype(BF16).reshape(N, N, W)

    def out_copy(k):
        peer = (me + k) % N
        return pltpu.make_async_remote_copy(
            src_ref=gated.at[peer],
            dst_ref=recv_out.at[me],
            send_sem=out_send.at[peer],
            recv_sem=out_recv.at[me],
            device_id={"seq": peer},
        )

    def out_arrival(k):
        peer = (me + k) % N
        return pltpu.make_async_remote_copy(
            src_ref=gated.at[peer],
            dst_ref=recv_out.at[peer],
            send_sem=out_send.at[peer],
            recv_sem=out_recv.at[peer],
            device_id={"seq": peer},
        )

    each(N, lambda k: out_copy(k).start())
    recv_out[me] = gated[me]

    @pl.when(column != 0)
    def _():
        tap_first().wait_send()

    each(N, lambda k: block_copy(k).wait_send())
    for t in range(3):
        each(N, lambda k: third_copy(t, k).wait_send())
    each(n_batch, lambda k: tap_copy(k).wait_send())
    each(N, lambda k: out_copy(k).wait_send())
    each(N, lambda k: out_arrival(k).wait_recv())
    whole = recv_out[...].reshape(W, W)
    out[...] = dot(whole, out_proj[...], ((0,), (0,))).astype(BF16)


def body(n_batch, events, positions, length, filters, skip_gain, short_filter, in_proj, out_proj):
    tables = [jnp.asarray(table) for table in make_tables()]
    inputs = [
        length.reshape(1, 1),
        positions.reshape(1, W),
        events,
        filters,
        skip_gain,
        short_filter,
        in_proj,
        out_proj,
        *tables,
    ]
    dma = lambda *shape: pltpu.SemaphoreType.DMA(shape)
    held = [pltpu.VMEM((W, 2, 128) if i == 3 else x.shape, x.dtype) for i, x in enumerate(inputs)]
    return pl.pallas_call(
        functools.partial(kernel, n_batch),
        out_shape=jax.ShapeDtypeStruct((W, W), BF16),
        in_specs=[pl.BlockSpec(memory_space=pl.ANY)] * INPUTS,
        out_specs=pl.BlockSpec(memory_space=pltpu.VMEM),
        scratch_shapes=held
        + [
            pltpu.VMEM((3, N, N, W), BF16),
            pltpu.VMEM((1, W), jnp.int32),
            pltpu.VMEM((N, W), BF16),
            pltpu.VMEM((N, N, W), BF16),
            pltpu.VMEM((3, N, N, W), BF16),
            pltpu.VMEM((N, 1, W), jnp.int32),
            pltpu.VMEM((2, N, N, W), BF16),
            pltpu.VMEM((N, N, W), BF16),
            pltpu.VMEM((2, W, 2 * W), F32),
            dma(INPUTS),
            dma(3, N),
            dma(3, N),
            dma(N),
            dma(N),
            dma(n_batch),
            dma(n_batch),
            pltpu.SemaphoreType.DMA,
            pltpu.SemaphoreType.DMA,
            dma(N),
            dma(N),
        ],
        compiler_params=pltpu.CompilerParams(
            collective_id=0, has_side_effects=True, vmem_limit_bytes=63 * 1024 * 1024
        ),
    )(*inputs)


def solution(mesh):
    return jax.shard_map(
        functools.partial(body, mesh.shape["batch"]),
        mesh=mesh,
        in_specs=(
            P(("batch", "seq"), None),
            P(("batch", "seq")),
            P("batch"),
            P("seq", None, None),
            P(),
            P(),
            P(),
            P(),
        ),
        out_specs=P(("batch", "seq"), None),
        check_vma=False,
    )
```

```python
import functools
import math

import jax
import jax.numpy as jnp
import ml_dtypes
import numpy as np
from jax import lax
from jax.experimental import pallas as pl
from jax.experimental.pallas import tpu as pltpu
from jax.sharding import PartitionSpec as P

N = 16
W = 256
POINTS = 2 * N * W
F32, BF16 = jnp.float32, jnp.bfloat16


def split(table):
    high = table.astype(ml_dtypes.bfloat16)
    low = (table - high.astype(np.float64)).astype(ml_dtypes.bfloat16)
    return high, low


@functools.cache
def make_tables():
    half = np.arange(N) + 0.5
    outer = 2 * np.pi * np.outer(half, np.arange(N)) / (2 * N)
    eye = np.eye(N)
    fwd_a = np.concatenate([np.kron(np.cos(outer), eye), np.kron(-np.sin(outer), eye)], 0)
    inv_a = np.concatenate([np.kron(np.cos(outer.T), eye), np.kron(-np.sin(outer.T), eye)], 1) * (2.0 / POINTS)
    inner = 2 * np.pi * (np.outer(np.arange(W), np.arange(W)) % W) / W
    cos, sin = np.cos(inner), np.sin(inner)
    fwd_b = np.block([[cos, -sin], [sin, cos]])
    inv_b = np.block([[cos, sin], [-sin, cos]])
    twist = 2 * np.pi * np.outer(half, np.arange(W)) / POINTS
    cat = lambda table, axis: np.concatenate([split(table)[i] for i in (0, 0, 1)], axis)
    return (
        cat(fwd_a, 1),
        cat(fwd_b, 0),
        cat(inv_b, 0),
        cat(inv_a, 1),
        np.stack([np.cos(twist), np.sin(twist)]).astype(np.float32),
    )


def parts(x, axis):
    high = x.astype(BF16)
    low = (x - high.astype(F32)).astype(BF16)
    return jnp.concatenate([high, low, high], axis=axis)


def dot(a, b, dims=((1,), (0,))):
    return lax.dot_general(a, b, (dims, ((), ())), preferred_element_type=F32)


INPUTS = 12


def kernel(n_batch, *refs):
    outside, (out, *inside), rest = refs[:INPUTS], refs[INPUTS : 2 * INPUTS + 1], refs[2 * INPUTS + 1 :]
    length, positions, events, filters, skip_gain, short_filter, in_proj, *tables = inside
    fwd_a, fwd_b, inv_b, inv_a, twist = tables
    (
        thirds,
        block_row,
        taps,
        gated,
        gate,
        passed,
        ids_row,
        recv_sig,
        recv_blk,
        recv_tap,
        spec,
        load_sem,
        sig_send,
        sig_recv,
        blk_send,
        blk_recv,
        tap_send,
        tap_recv,
        own_send,
        own_recv,
        twin_send,
        twin_recv,
        keep_sem,
        out_send,
        out_recv,
    ) = rest
    me = lax.axis_index("seq")
    lane = lax.axis_index("batch")
    column, core = lane // 2, lane % 2
    chips, sibling = n_batch // 2, column * 2 + 1 - core

    target = (me + column) % N
    loads = []
    for i, (src, dst) in enumerate(zip(outside, inside)):
        if i == 3:
            src = src.at[:, :, pl.ds(pl.multiple_of(target // 8 * 128, 128), 128)]
        loads.append(pltpu.make_async_copy(src, dst, load_sem.at[i]))
    for i in (1, 2, 6, 0, 3, 7, 11, 8, 5, 4, 9, 10):
        loads[i].start()

    barrier = pltpu.get_barrier_semaphore()

    def greet(k, carry):
        pl.semaphore_signal(barrier, inc=1, device_id={"seq": (me + k) % N})
        return carry

    def greet_plane(k, carry):
        pl.semaphore_signal(barrier, inc=1, device_id={"batch": (lane + 2 * k) % n_batch})
        return carry

    lax.fori_loop(1, N, greet, 0)
    lax.fori_loop(1, chips, greet_plane, 0)
    pl.semaphore_signal(barrier, inc=1, device_id={"batch": sibling})

    for i in (1, 0, 2, 6):
        loads[i].wait()
    pos = positions[...]
    order = lax.broadcasted_iota(jnp.int32, (W, W), 0) == pos % W
    one_hot = order.astype(BF16)
    kept = jnp.where(pos < length[...], one_hot, jnp.zeros_like(one_hot))
    ids = jnp.broadcast_to((pos // W).astype(BF16), (N, W))
    block_row[...] = dot(ids, one_hot, ((1,), (1,)))[0:1].astype(jnp.int32)
    ordered = dot(kept, events[...]).astype(BF16)

    def project(t):
        projected = dot(ordered, in_proj[:, t * W : (t + 1) * W])
        thirds[:, t] = projected.T.astype(BF16).reshape(N, N, W)

    project(0)
    loads[3].wait()
    rows16 = lax.broadcasted_iota(jnp.int32, (N, W), 0)
    lanes16 = lax.broadcasted_iota(jnp.int32, (N, W), 1)
    pick = (lanes16[:, :128] == rows16[:, :128] + target % 8 * N).astype(BF16)
    lags = jnp.where(core == 0, filters[:, 0, :], filters[:, 1, :]).astype(BF16)
    taps[...] = dot(pick, lags, ((1,), (1,))).astype(BF16)
    pl.semaphore_wait(barrier, N - 1 + chips)

    def tap_first():
        return pltpu.make_async_remote_copy(
            src_ref=taps,
            dst_ref=recv_tap.at[core, me],
            send_sem=own_send,
            recv_sem=own_recv,
            device_id={"seq": target},
        )

    slot = (me + N - column) % N

    def block_copy(k):
        peer = (me + k) % N
        return pltpu.make_async_remote_copy(
            src_ref=block_row,
            dst_ref=recv_blk.at[me],
            send_sem=blk_send.at[peer],
            recv_sem=blk_recv.at[me],
            device_id={"seq": peer},
        )

    def block_arrival(k):
        peer = (me + k) % N
        return pltpu.make_async_remote_copy(
            src_ref=block_row,
            dst_ref=recv_blk.at[peer],
            send_sem=blk_send.at[peer],
            recv_sem=blk_recv.at[peer],
            device_id={"seq": peer},
        )

    def sent(part):
        return pl.ds(0, 1) if part == 0 else pl.ds(1, 2)

    def third_copy(part, k):
        peer = (me + k) % N
        return pltpu.make_async_remote_copy(
            src_ref=thirds.at[peer, sent(part)],
            dst_ref=recv_sig.at[me, sent(part)],
            send_sem=sig_send.at[part, peer],
            recv_sem=sig_recv.at[part, me],
            device_id={"seq": peer},
        )

    def third_arrival(part, k):
        peer = (me + k) % N
        return pltpu.make_async_remote_copy(
            src_ref=thirds.at[peer, sent(part)],
            dst_ref=recv_sig.at[peer, sent(part)],
            send_sem=sig_send.at[part, peer],
            recv_sem=sig_recv.at[part, peer],
            device_id={"seq": peer},
        )

    def each(count, act):
        def step(k, carry):
            act(k)
            return carry

        lax.fori_loop(1, count, step, 0)

    @pl.when(column != 0)
    def _():
        tap_first().start()

    @pl.when(column == 0)
    def _():
        recv_tap[core, me] = taps[...]

    each(N, lambda k: block_copy(k).start())
    each(N, lambda k: third_copy(0, k).start())
    recv_blk[me] = block_row[...]
    project(1)
    project(2)
    recv_sig[me] = thirds[me]

    @pl.when(column != 0)
    def _():
        pltpu.make_async_remote_copy(
            src_ref=taps,
            dst_ref=recv_tap.at[core, slot],
            send_sem=own_send,
            recv_sem=own_recv,
            device_id={"seq": target},
        ).wait_recv()

    def tap_copy(k):
        peer = (column + k) % chips
        return pltpu.make_async_remote_copy(
            src_ref=recv_tap.at[core, slot],
            dst_ref=recv_tap.at[core, slot],
            send_sem=tap_send.at[peer],
            recv_sem=tap_recv.at[column],
            device_id={"batch": peer * 2 + core},
        )

    def tap_arrival(k):
        peer = (column + k) % chips
        there = recv_tap.at[core, (me + N - peer) % N]
        return pltpu.make_async_remote_copy(
            src_ref=there,
            dst_ref=there,
            send_sem=tap_send.at[peer],
            recv_sem=tap_recv.at[peer],
            device_id={"batch": peer * 2 + core},
        )

    def twin_copy(which):
        return pltpu.make_async_remote_copy(
            src_ref=recv_tap.at[which],
            dst_ref=recv_tap.at[which],
            send_sem=twin_send,
            recv_sem=twin_recv,
            device_id={"batch": sibling},
        )

    each(chips, lambda k: tap_copy(k).start())
    each(N, lambda k: third_copy(1, k).start())

    def column_of(row):
        return jnp.sum(jnp.where(lanes16 == rows16 + me * N, row, 0.0), axis=1, keepdims=True)[None]

    def rotate(re, im, sign):
        cos = twist[0][:, None, :]
        sin = twist[1][:, None, :] * sign
        re, im = re.reshape(N, N, W), im.reshape(N, N, W)
        return (re * cos + im * sin).reshape(W, W), (im * cos - re * sin).reshape(W, W)

    def forward(signal):
        mid = dot(fwd_a[...], parts(signal, 0))
        re, im = rotate(mid[:W], mid[W:], 1.0)
        return dot(parts(jnp.concatenate([re, im], axis=1), 1), fwd_b[...])

    def filtered(got, f):
        re, im = got[:, :W], got[:, W:]
        tap_re, tap_im = spec[f, :, :W], spec[f, :, W:]
        re, im = re * tap_re - im * tap_im, re * tap_im + im * tap_re
        mid = dot(parts(jnp.concatenate([re, im], axis=1), 1), inv_b[...])
        re, im = rotate(mid[:, :W], mid[:, W:], -1.0)
        return parts(jnp.concatenate([re, im], axis=0), 0)

    sub = lax.broadcasted_iota(jnp.int32, (W, W), 1)

    def short(t):
        rows = []
        for b in range(N):
            total = jnp.zeros((N, W), BF16)
            for s in range(N):
                total = jnp.where(ids_row[s] == b, recv_sig[s, t], total)
            rows.append(total)
        stream = jnp.concatenate(rows, axis=0).astype(F32)
        before = jnp.concatenate([jnp.zeros((N, W), F32), stream[:-N]], axis=0)
        one = pltpu.roll(jnp.where(sub == W - 1, before, stream), 1, 1)
        two = pltpu.roll(jnp.where(sub >= W - 2, before, stream), 2, 1)
        tap = [column_of(short_filter[i : i + 1, t * W : (t + 1) * W]) for i in range(3)]
        blocks = lambda x: x.reshape(N, N, W)
        return (tap[0] * blocks(stream) + tap[1] * blocks(one) + tap[2] * blocks(two)).reshape(W, W)

    each(chips, lambda k: tap_arrival(k).wait_recv())
    twin_copy(core).start()
    for i in (7, 11, 8, 5, 4):
        loads[i].wait()
    gain = [column_of(skip_gain[i : i + 1, :]) for i in range(2)]
    scaled = lambda g, x: (g * x.reshape(-1, N, W)).reshape(-1, W)

    each(N, lambda k: block_arrival(k).wait_recv())
    for s in range(N):
        ids_row[s] = jnp.broadcast_to(recv_blk[s].astype(F32), (N, W)).astype(BF16)
    each(N, lambda k: third_arrival(0, k).wait_recv())
    value = short(0)
    ahead = forward(value)
    twin_copy(1 - core).wait_recv()
    spec[0] = forward(recv_tap[0].reshape(W, W).astype(F32))
    for i in (9, 10):
        loads[i].wait()
    first = dot(inv_a[...], filtered(ahead, 0)) + scaled(gain[0], value)
    spec[1] = forward(recv_tap[1].reshape(W, W).astype(F32))
    each(N, lambda k: third_arrival(1, k).wait_recv())
    first = short(1) * first
    gate[...] = short(2)
    passed[...] = scaled(gain[1], first)
    ahead = filtered(forward(first), 1)
    def out_copy(k):
        peer = (me + k) % N
        return pltpu.make_async_remote_copy(
            src_ref=gated.at[peer],
            dst_ref=out.at[me],
            send_sem=out_send.at[peer],
            recv_sem=out_recv.at[me],
            device_id={"seq": peer},
        )

    def out_arrival(k):
        peer = (me + k) % N
        return pltpu.make_async_remote_copy(
            src_ref=gated.at[peer],
            dst_ref=out.at[peer],
            send_sem=out_send.at[peer],
            recv_sem=out_recv.at[peer],
            device_id={"seq": peer},
        )

    for g in range(4):
        group = (me // 4 + g) % 4
        at = pl.ds(pl.multiple_of(group * 64, 64), 64)
        rows = gate[at, :] * (dot(inv_a[at, :], ahead) + passed[at, :])
        gated[pl.ds(group * 4, 4)] = rows.astype(BF16).reshape(4, N, W)
        for i in range(4):
            peer = group * 4 + i

            @pl.when(peer != me)
            def _():
                out_copy((peer + N - me) % N).start()

    own = pltpu.make_async_copy(gated.at[me], out.at[me], keep_sem)
    own.start()

    @pl.when(column != 0)
    def _():
        tap_first().wait_send()

    each(N, lambda k: block_copy(k).wait_send())
    for part in range(2):
        each(N, lambda k: third_copy(part, k).wait_send())
    each(chips, lambda k: tap_copy(k).wait_send())
    twin_copy(core).wait_send()
    each(N, lambda k: out_copy(k).wait_send())
    each(N, lambda k: out_arrival(k).wait_recv())
    own.wait()


def body(n_batch, events, positions, length, filters, skip_gain, short_filter, in_proj, out_proj):
    tables = [jnp.asarray(table) for table in make_tables()]
    inputs = [
        length.reshape(1, 1),
        positions.reshape(1, W),
        events,
        filters,
        skip_gain,
        short_filter,
        in_proj,
        *tables,
    ]
    dma = lambda *shape: pltpu.SemaphoreType.DMA(shape)
    held = [pltpu.VMEM((W, 2, 128) if i == 3 else x.shape, x.dtype) for i, x in enumerate(inputs)]
    gated = pl.pallas_call(
        functools.partial(kernel, n_batch),
        out_shape=jax.ShapeDtypeStruct((N, N, W), BF16),
        in_specs=[pl.BlockSpec(memory_space=pl.ANY)] * INPUTS,
        out_specs=pl.BlockSpec(memory_space=pl.ANY),
        scratch_shapes=held
        + [
            pltpu.VMEM((N, 3, N, W), BF16),
            pltpu.VMEM((1, W), jnp.int32),
            pltpu.VMEM((N, W), BF16),
            pltpu.VMEM((N, N, W), BF16),
            pltpu.VMEM((W, W), F32),
            pltpu.VMEM((W, W), F32),
            pltpu.VMEM((N, N, W), BF16),
            pltpu.VMEM((N, 3, N, W), BF16),
            pltpu.VMEM((N, 1, W), jnp.int32),
            pltpu.VMEM((2, N, N, W), BF16),
            pltpu.VMEM((2, W, 2 * W), F32),
            dma(INPUTS),
            dma(2, N),
            dma(2, N),
            dma(N),
            dma(N),
            dma(n_batch // 2),
            dma(n_batch // 2),
            pltpu.SemaphoreType.DMA,
            pltpu.SemaphoreType.DMA,
            pltpu.SemaphoreType.DMA,
            pltpu.SemaphoreType.DMA,
            pltpu.SemaphoreType.DMA,
            dma(N),
            dma(N),
        ],
        compiler_params=pltpu.CompilerParams(
            collective_id=0, has_side_effects=True, vmem_limit_bytes=63 * 1024 * 1024
        ),
    )(*inputs)
    return dot(gated.reshape(W, W), out_proj, ((0,), (0,))).astype(BF16)


def solution(mesh):
    return jax.shard_map(
        functools.partial(body, mesh.shape["batch"]),
        mesh=mesh,
        in_specs=(
            P(("batch", "seq"), None),
            P(("batch", "seq")),
            P("batch"),
            P("seq", None, None),
            P(),
            P(),
            P(),
            P(),
        ),
        out_specs=P(("batch", "seq"), None),
        check_vma=False,
    )
```

```python
import functools
import math

import jax
import jax.numpy as jnp
import ml_dtypes
import numpy as np
from jax import lax
from jax.experimental import pallas as pl
from jax.experimental.pallas import tpu as pltpu
from jax.sharding import PartitionSpec as P

N = 16
FAR = (8, 7, 9, 6, 10, 5, 11, 4, 12, 3, 13, 2, 14, 1, 15)
W = 256
POINTS = 2 * N * W
F32, BF16 = jnp.float32, jnp.bfloat16


def split(table):
    high = table.astype(ml_dtypes.bfloat16)
    low = (table - high.astype(np.float64)).astype(ml_dtypes.bfloat16)
    return high, low


@functools.cache
def make_tables():
    half = np.arange(N) + 0.5
    outer = 2 * np.pi * np.outer(half, np.arange(N)) / (2 * N)
    eye = np.eye(N)
    fwd_a = np.concatenate([np.kron(np.cos(outer), eye), np.kron(-np.sin(outer), eye)], 0)
    inv_a = np.concatenate([np.kron(np.cos(outer.T), eye), np.kron(-np.sin(outer.T), eye)], 1) * (2.0 / POINTS)
    inner = 2 * np.pi * (np.outer(np.arange(W), np.arange(W)) % W) / W
    cos, sin = np.cos(inner), np.sin(inner)
    fwd_b = np.block([[cos, -sin], [sin, cos]])
    inv_b = np.block([[cos, sin], [-sin, cos]])
    twist = 2 * np.pi * np.outer(half, np.arange(W)) / POINTS
    cat = lambda table, axis: np.concatenate([split(table)[i] for i in (0, 0, 1)], axis)
    return (
        cat(fwd_a, 1),
        cat(fwd_b, 0),
        cat(inv_b, 0),
        cat(inv_a, 1),
        np.stack([np.cos(twist), np.sin(twist)]).astype(np.float32),
    )


def parts(x, axis):
    high = x.astype(BF16)
    low = (x - high.astype(F32)).astype(BF16)
    return jnp.concatenate([high, low, high], axis=axis)


def dot(a, b, dims=((1,), (0,))):
    return lax.dot_general(a, b, (dims, ((), ())), preferred_element_type=F32)


INPUTS = 12


def kernel(n_batch, *refs):
    outside, (out, *inside), rest = refs[:INPUTS], refs[INPUTS : 2 * INPUTS + 1], refs[2 * INPUTS + 1 :]
    length, positions, events, filters, skip_gain, short_filter, in_proj, *tables = inside
    fwd_a, fwd_b, inv_b, inv_a, twist = tables
    (
        thirds,
        block_row,
        taps,
        gated,
        gate,
        passed,
        ids_row,
        recv_sig,
        recv_blk,
        recv_tap,
        spec,
        load_sem,
        sig_send,
        sig_recv,
        blk_send,
        blk_recv,
        tap_send,
        tap_recv,
        own_send,
        own_recv,
        keep_sem,
        out_send,
        out_recv,
    ) = rest
    me = lax.axis_index("seq")
    lane = lax.axis_index("batch")
    column, core = lane // 2, lane % 2
    chips = n_batch // 2
    target = (me + column) % N

    barrier = pltpu.get_barrier_semaphore()
    for k in FAR:
        pl.semaphore_signal(barrier, inc=1, device_id={"seq": (me + k) % N})
    loads = []
    for i, (src, dst) in enumerate(zip(outside, inside)):
        if i == 3:
            src = src.at[:, :, pl.ds(pl.multiple_of(target // 8 * 128, 128), 128)]
        loads.append(pltpu.make_async_copy(src, dst, load_sem.at[i]))
    for i in (1, 2, 6, 0, 3):
        loads[i].start()
    for k in range(1, chips):
        pl.semaphore_signal(barrier, inc=1, device_id={"batch": (lane + 2 * k) % n_batch})
    for i in (7, 11, 8, 5, 4, 9, 10):
        loads[i].start()

    for i in (1, 0, 2, 6):
        loads[i].wait()
    pos = positions[...]
    order = lax.broadcasted_iota(jnp.int32, (W, W), 0) == pos % W
    one_hot = order.astype(BF16)
    kept = jnp.where(pos < length[...], one_hot, jnp.zeros_like(one_hot))
    ids = jnp.broadcast_to((pos // W).astype(BF16), (N, W))
    block_row[...] = dot(ids, one_hot, ((1,), (1,)))[0:1].astype(jnp.int32)
    ordered = dot(kept, events[...]).astype(BF16)

    def project(t):
        projected = dot(ordered, in_proj[:, t * W : (t + 1) * W])
        thirds[:, t] = projected.T.astype(BF16).reshape(N, N, W)

    project(0)
    project(1)
    project(2)
    loads[3].wait()
    rows16 = lax.broadcasted_iota(jnp.int32, (N, W), 0)
    lanes16 = lax.broadcasted_iota(jnp.int32, (N, W), 1)
    pick = (lanes16[:, :128] == rows16[:, :128] + target % 8 * N).astype(BF16)
    for f in range(2):
        taps[f] = dot(pick, filters[:, f, :].astype(BF16), ((1,), (1,))).astype(BF16)
    pl.semaphore_wait(barrier, N - 1 + chips - 1)

    def tap_first():
        return pltpu.make_async_remote_copy(
            src_ref=taps,
            dst_ref=recv_tap.at[me],
            send_sem=own_send,
            recv_sem=own_recv,
            device_id={"seq": target},
        )

    slot = (me + N - column) % N

    def block_copy(k):
        peer = (me + k) % N
        return pltpu.make_async_remote_copy(
            src_ref=block_row,
            dst_ref=recv_blk.at[me],
            send_sem=blk_send.at[peer],
            recv_sem=blk_recv.at[me],
            device_id={"seq": peer},
        )

    def block_arrival(k):
        peer = (me + k) % N
        return pltpu.make_async_remote_copy(
            src_ref=block_row,
            dst_ref=recv_blk.at[peer],
            send_sem=blk_send.at[peer],
            recv_sem=blk_recv.at[peer],
            device_id={"seq": peer},
        )

    def third_copy(part, k):
        peer = (me + k) % N
        return pltpu.make_async_remote_copy(
            src_ref=thirds.at[peer, part],
            dst_ref=recv_sig.at[me, part],
            send_sem=sig_send.at[part, peer],
            recv_sem=sig_recv.at[part, me],
            device_id={"seq": peer},
        )

    def third_arrival(part, k):
        peer = (me + k) % N
        return pltpu.make_async_remote_copy(
            src_ref=thirds.at[peer, part],
            dst_ref=recv_sig.at[peer, part],
            send_sem=sig_send.at[part, peer],
            recv_sem=sig_recv.at[part, peer],
            device_id={"seq": peer},
        )

    def each(count, act):
        def step(k, carry):
            act(k)
            return carry

        lax.fori_loop(1, count, step, 0)

    @pl.when(column != 0)
    def _():
        tap_first().start()

    @pl.when(column == 0)
    def _():
        recv_tap[me] = taps[...]

    for k in FAR:
        block_copy(k).start()
        third_copy(0, k).start()
    for part in (1, 2):
        for k in FAR:
            third_copy(part, k).start()
    recv_blk[me] = block_row[...]
    recv_sig[me] = thirds[me]

    @pl.when(column != 0)
    def _():
        pltpu.make_async_remote_copy(
            src_ref=taps,
            dst_ref=recv_tap.at[slot],
            send_sem=own_send,
            recv_sem=own_recv,
            device_id={"seq": target},
        ).wait_recv()

    def tap_copy(k):
        peer = (column + k) % chips
        return pltpu.make_async_remote_copy(
            src_ref=recv_tap.at[slot],
            dst_ref=recv_tap.at[slot],
            send_sem=tap_send.at[peer],
            recv_sem=tap_recv.at[column],
            device_id={"batch": peer * 2 + core},
        )

    def tap_arrival(k):
        peer = (column + k) % chips
        there = recv_tap.at[(me + N - peer) % N]
        return pltpu.make_async_remote_copy(
            src_ref=there,
            dst_ref=there,
            send_sem=tap_send.at[peer],
            recv_sem=tap_recv.at[peer],
            device_id={"batch": peer * 2 + core},
        )

    for k in range(1, chips):
        tap_copy(k).start()

    def column_of(row):
        return jnp.sum(jnp.where(lanes16 == rows16 + me * N, row, 0.0), axis=1, keepdims=True)[None]

    def rotate(re, im, sign):
        cos = twist[0][:, None, :]
        sin = twist[1][:, None, :] * sign
        re, im = re.reshape(N, N, W), im.reshape(N, N, W)
        return (re * cos + im * sin).reshape(W, W), (im * cos - re * sin).reshape(W, W)

    def forward(signal):
        mid = dot(fwd_a[...], parts(signal, 0))
        re, im = rotate(mid[:W], mid[W:], 1.0)
        return dot(parts(jnp.concatenate([re, im], axis=1), 1), fwd_b[...])

    def filtered(got, f):
        re, im = got[:, :W], got[:, W:]
        tap_re, tap_im = spec[f, :, :W], spec[f, :, W:]
        re, im = re * tap_re - im * tap_im, re * tap_im + im * tap_re
        mid = dot(parts(jnp.concatenate([re, im], axis=1), 1), inv_b[...])
        re, im = rotate(mid[:, :W], mid[:, W:], -1.0)
        return parts(jnp.concatenate([re, im], axis=0), 0)

    sub = lax.broadcasted_iota(jnp.int32, (W, W), 1)

    def short(t):
        rows = []
        for b in range(N):
            total = jnp.zeros((N, W), BF16)
            for s in range(N):
                total = jnp.where(ids_row[s] == b, recv_sig[s, t], total)
            rows.append(total)
        stream = jnp.concatenate(rows, axis=0).astype(F32)
        before = jnp.concatenate([jnp.zeros((N, W), F32), stream[:-N]], axis=0)
        one = pltpu.roll(jnp.where(sub == W - 1, before, stream), 1, 1)
        two = pltpu.roll(jnp.where(sub >= W - 2, before, stream), 2, 1)
        tap = [column_of(short_filter[i : i + 1, t * W : (t + 1) * W]) for i in range(3)]
        blocks = lambda x: x.reshape(N, N, W)
        return (tap[0] * blocks(stream) + tap[1] * blocks(one) + tap[2] * blocks(two)).reshape(W, W)

    for i in (7, 11, 8, 5, 4, 9, 10):
        loads[i].wait()
    gain = [column_of(skip_gain[i : i + 1, :]) for i in range(2)]
    scaled = lambda g, x: (g * x.reshape(-1, N, W)).reshape(-1, W)
    spectrum = lambda f: forward(recv_tap[:, f].reshape(W, W).astype(F32))

    each(N, lambda k: block_arrival(k).wait_recv())
    for s in range(N):
        ids_row[s] = jnp.broadcast_to(recv_blk[s].astype(F32), (N, W)).astype(BF16)
    each(N, lambda k: third_arrival(0, k).wait_recv())
    value = short(0)
    ahead = forward(value)
    each(N, lambda k: third_arrival(1, k).wait_recv())
    gate[...] = short(1)
    each(chips, lambda k: tap_arrival(k).wait_recv())
    spec[0] = spectrum(0)
    first = gate[...] * (dot(inv_a[...], filtered(ahead, 0)) + scaled(gain[0], value))
    passed[...] = scaled(gain[1], first)
    spec[1] = spectrum(1)
    ahead = filtered(forward(first), 1)
    each(N, lambda k: third_arrival(2, k).wait_recv())
    gate[...] = short(2)

    def out_copy(k):
        peer = (me + k) % N
        return pltpu.make_async_remote_copy(
            src_ref=gated.at[peer],
            dst_ref=out.at[me],
            send_sem=out_send.at[peer],
            recv_sem=out_recv.at[me],
            device_id={"seq": peer},
        )

    def out_arrival(k):
        peer = (me + k) % N
        return pltpu.make_async_remote_copy(
            src_ref=gated.at[peer],
            dst_ref=out.at[peer],
            send_sem=out_send.at[peer],
            recv_sem=out_recv.at[peer],
            device_id={"seq": peer},
        )

    for g in (2, 1, 3, 0):
        group = (me // 4 + g) % 4
        at = pl.ds(pl.multiple_of(group * 64, 64), 64)
        rows = gate[at, :] * (dot(inv_a[at, :], ahead) + passed[at, :])
        gated[pl.ds(group * 4, 4)] = rows.astype(BF16).reshape(4, N, W)
        for i in range(4):
            peer = group * 4 + i

            @pl.when(peer != me)
            def _():
                out_copy((peer + N - me) % N).start()

    own = pltpu.make_async_copy(gated.at[me], out.at[me], keep_sem)
    own.start()

    @pl.when(column != 0)
    def _():
        tap_first().wait_send()

    each(N, lambda k: block_copy(k).wait_send())
    for part in range(3):
        each(N, lambda k: third_copy(part, k).wait_send())
    each(chips, lambda k: tap_copy(k).wait_send())
    each(N, lambda k: out_copy(k).wait_send())
    each(N, lambda k: out_arrival(k).wait_recv())
    own.wait()


def body(n_batch, events, positions, length, filters, skip_gain, short_filter, in_proj, out_proj):
    tables = [jnp.asarray(table) for table in make_tables()]
    inputs = [
        length.reshape(1, 1),
        positions.reshape(1, W),
        events,
        filters,
        skip_gain,
        short_filter,
        in_proj,
        *tables,
    ]
    dma = lambda *shape: pltpu.SemaphoreType.DMA(shape)
    held = [pltpu.VMEM((W, 2, 128) if i == 3 else x.shape, x.dtype) for i, x in enumerate(inputs)]
    gated = pl.pallas_call(
        functools.partial(kernel, n_batch),
        out_shape=jax.ShapeDtypeStruct((N, N, W), BF16),
        in_specs=[pl.BlockSpec(memory_space=pl.ANY)] * INPUTS,
        out_specs=pl.BlockSpec(memory_space=pl.ANY),
        scratch_shapes=held
        + [
            pltpu.VMEM((N, 3, N, W), BF16),
            pltpu.VMEM((1, W), jnp.int32),
            pltpu.VMEM((2, N, W), BF16),
            pltpu.VMEM((N, N, W), BF16),
            pltpu.VMEM((W, W), F32),
            pltpu.VMEM((W, W), F32),
            pltpu.VMEM((N, N, W), BF16),
            pltpu.VMEM((N, 3, N, W), BF16),
            pltpu.VMEM((N, 1, W), jnp.int32),
            pltpu.VMEM((N, 2, N, W), BF16),
            pltpu.VMEM((2, W, 2 * W), F32),
            dma(INPUTS),
            dma(3, N),
            dma(3, N),
            dma(N),
            dma(N),
            dma(n_batch // 2),
            dma(n_batch // 2),
            pltpu.SemaphoreType.DMA,
            pltpu.SemaphoreType.DMA,
            pltpu.SemaphoreType.DMA,
            dma(N),
            dma(N),
        ],
        compiler_params=pltpu.CompilerParams(
            collective_id=0, has_side_effects=True, vmem_limit_bytes=63 * 1024 * 1024
        ),
    )(*inputs)
    return dot(gated.reshape(W, W), out_proj, ((0,), (0,))).astype(BF16)


def solution(mesh):
    return jax.shard_map(
        functools.partial(body, mesh.shape["batch"]),
        mesh=mesh,
        in_specs=(
            P(("batch", "seq"), None),
            P(("batch", "seq")),
            P("batch"),
            P("seq", None, None),
            P(),
            P(),
            P(),
            P(),
        ),
        out_specs=P(("batch", "seq"), None),
        check_vma=False,
    )
```

```python
import functools
import math

import jax
import jax.numpy as jnp
import ml_dtypes
import numpy as np
from jax import lax
from jax.experimental import pallas as pl
from jax.experimental.pallas import tpu as pltpu
from jax.sharding import PartitionSpec as P

N = 16
FAR = (8, 7, 9, 6, 10, 5, 11, 4, 12, 3, 13, 2, 14, 1, 15)
W = 256
POINTS = 2 * N * W
F32, BF16 = jnp.float32, jnp.bfloat16


def split(table):
    high = table.astype(ml_dtypes.bfloat16)
    low = (table - high.astype(np.float64)).astype(ml_dtypes.bfloat16)
    return high, low


@functools.cache
def make_tables():
    half = np.arange(N) + 0.5
    outer = 2 * np.pi * np.outer(half, np.arange(N)) / (2 * N)
    eye = np.eye(N)
    fwd_a = np.concatenate([np.kron(np.cos(outer), eye), np.kron(-np.sin(outer), eye)], 0)
    inv_a = np.concatenate([np.kron(np.cos(outer.T), eye), np.kron(-np.sin(outer.T), eye)], 1) * (2.0 / POINTS)
    inner = 2 * np.pi * (np.outer(np.arange(W), np.arange(W)) % W) / W
    cos, sin = np.cos(inner), np.sin(inner)
    fwd_b = np.block([[cos, -sin], [sin, cos]])
    inv_b = np.block([[cos, sin], [-sin, cos]])
    twist = 2 * np.pi * np.outer(half, np.arange(W)) / POINTS
    cat = lambda table, axis, order=(0, 0, 1): np.concatenate([split(table)[i] for i in order], axis)
    return (
        cat(fwd_a, 1),
        cat(fwd_b, 0, (0, 1)),
        cat(inv_b, 0, (0, 1)),
        cat(inv_a, 1),
        np.stack([np.cos(twist), np.sin(twist)]).astype(np.float32),
    )


def parts(x, axis):
    high = x.astype(BF16)
    low = (x - high.astype(F32)).astype(BF16)
    return jnp.concatenate([high, low, high], axis=axis)


def dot(a, b, dims=((1,), (0,))):
    return lax.dot_general(a, b, (dims, ((), ())), preferred_element_type=F32)


INPUTS = 12


def kernel(n_batch, *refs):
    outside, (out, *inside), rest = refs[:INPUTS], refs[INPUTS : 2 * INPUTS + 1], refs[2 * INPUTS + 1 :]
    length, positions, events, filters, skip_gain, short_filter, in_proj, *tables = inside
    fwd_a, fwd_b, inv_b, inv_a, twist = tables
    (
        thirds,
        block_row,
        taps,
        gated,
        gate,
        passed,
        ids_row,
        recv_sig,
        recv_blk,
        recv_tap,
        spec,
        load_sem,
        sig_send,
        sig_recv,
        blk_send,
        blk_recv,
        tap_send,
        tap_recv,
        own_send,
        own_recv,
        keep_sem,
        out_send,
        out_recv,
    ) = rest
    me = lax.axis_index("seq")
    lane = lax.axis_index("batch")
    column, core = lane // 2, lane % 2
    chips = n_batch // 2
    target = (me + column) % N

    barrier = pltpu.get_barrier_semaphore()
    for k in FAR:
        pl.semaphore_signal(barrier, inc=1, device_id={"seq": (me + k) % N})
    loads = []
    for i, (src, dst) in enumerate(zip(outside, inside)):
        if i == 3:
            src = src.at[:, :, pl.ds(pl.multiple_of(target // 8 * 128, 128), 128)]
        loads.append(pltpu.make_async_copy(src, dst, load_sem.at[i]))
    for i in (1, 2, 6, 0, 3):
        loads[i].start()
    for k in range(1, chips):
        pl.semaphore_signal(barrier, inc=1, device_id={"batch": (lane + 2 * k) % n_batch})
    for i in (7, 11, 8, 5, 4, 9, 10):
        loads[i].start()

    for i in (1, 0, 2, 6):
        loads[i].wait()
    pos = positions[...]
    order = lax.broadcasted_iota(jnp.int32, (W, W), 0) == pos % W
    one_hot = order.astype(BF16)
    kept = jnp.where(pos < length[...], one_hot, jnp.zeros_like(one_hot))
    ids = jnp.broadcast_to((pos // W).astype(BF16), (N, W))
    block_row[...] = dot(ids, one_hot, ((1,), (1,)))[0:1].astype(jnp.int32)
    ordered = dot(kept, events[...]).astype(BF16)

    def project(t):
        projected = dot(ordered, in_proj[:, t * W : (t + 1) * W])
        thirds[:, t] = projected.T.astype(BF16).reshape(N, N, W)

    project(0)
    project(1)
    project(2)
    loads[3].wait()
    rows16 = lax.broadcasted_iota(jnp.int32, (N, W), 0)
    lanes16 = lax.broadcasted_iota(jnp.int32, (N, W), 1)
    pick = (lanes16[:, :128] == rows16[:, :128] + target % 8 * N).astype(BF16)
    for f in range(2):
        taps[f] = dot(pick, filters[:, f, :].astype(BF16), ((1,), (1,))).astype(BF16)
    pl.semaphore_wait(barrier, N - 1 + chips - 1)

    def tap_first():
        return pltpu.make_async_remote_copy(
            src_ref=taps,
            dst_ref=recv_tap.at[me],
            send_sem=own_send,
            recv_sem=own_recv,
            device_id={"seq": target},
        )

    slot = (me + N - column) % N

    def block_copy(k):
        peer = (me + k) % N
        return pltpu.make_async_remote_copy(
            src_ref=block_row,
            dst_ref=recv_blk.at[me],
            send_sem=blk_send.at[peer],
            recv_sem=blk_recv.at[me],
            device_id={"seq": peer},
        )

    def block_arrival(k):
        peer = (me + k) % N
        return pltpu.make_async_remote_copy(
            src_ref=block_row,
            dst_ref=recv_blk.at[peer],
            send_sem=blk_send.at[peer],
            recv_sem=blk_recv.at[peer],
            device_id={"seq": peer},
        )

    def third_copy(part, k):
        peer = (me + k) % N
        return pltpu.make_async_remote_copy(
            src_ref=thirds.at[peer, part],
            dst_ref=recv_sig.at[me, part],
            send_sem=sig_send.at[part, peer],
            recv_sem=sig_recv.at[part, me],
            device_id={"seq": peer},
        )

    def third_arrival(part, k):
        peer = (me + k) % N
        return pltpu.make_async_remote_copy(
            src_ref=thirds.at[peer, part],
            dst_ref=recv_sig.at[peer, part],
            send_sem=sig_send.at[part, peer],
            recv_sem=sig_recv.at[part, peer],
            device_id={"seq": peer},
        )

    def each(count, act):
        def step(k, carry):
            act(k)
            return carry

        lax.fori_loop(1, count, step, 0)

    @pl.when(column != 0)
    def _():
        tap_first().start()

    @pl.when(column == 0)
    def _():
        recv_tap[me] = taps[...]

    for k in FAR:
        block_copy(k).start()
        third_copy(0, k).start()
    for k in FAR:
        third_copy(1, k).start()
    recv_blk[me] = block_row[...]
    recv_sig[me] = thirds[me]

    @pl.when(column != 0)
    def _():
        pltpu.make_async_remote_copy(
            src_ref=taps,
            dst_ref=recv_tap.at[slot],
            send_sem=own_send,
            recv_sem=own_recv,
            device_id={"seq": target},
        ).wait_recv()

    def tap_copy(k):
        peer = (column + k) % chips
        return pltpu.make_async_remote_copy(
            src_ref=recv_tap.at[slot],
            dst_ref=recv_tap.at[slot],
            send_sem=tap_send.at[peer],
            recv_sem=tap_recv.at[column],
            device_id={"batch": peer * 2 + core},
        )

    def tap_arrival(k):
        peer = (column + k) % chips
        there = recv_tap.at[(me + N - peer) % N]
        return pltpu.make_async_remote_copy(
            src_ref=there,
            dst_ref=there,
            send_sem=tap_send.at[peer],
            recv_sem=tap_recv.at[peer],
            device_id={"batch": peer * 2 + core},
        )

    for k in range(1, chips):
        tap_copy(k).start()
    for k in FAR:
        third_copy(2, k).start()

    def column_of(row):
        return jnp.sum(jnp.where(lanes16 == rows16 + me * N, row, 0.0), axis=1, keepdims=True)[None]

    def rotate(re, im, sign):
        cos = twist[0][:, None, :]
        sin = twist[1][:, None, :] * sign
        re, im = re.reshape(N, N, W), im.reshape(N, N, W)
        return (re * cos + im * sin).reshape(W, W), (im * cos - re * sin).reshape(W, W)

    def inner(re, im, table):
        x = jnp.concatenate([re, im], axis=1).astype(BF16)
        return dot(jnp.concatenate([x, x], axis=1), table[...])

    def forward(signal):
        if signal.dtype == BF16:
            mid = dot(fwd_a[:, W:], jnp.concatenate([signal, signal], axis=0))
        else:
            mid = dot(fwd_a[...], parts(signal, 0))
        re, im = rotate(mid[:W], mid[W:], 1.0)
        return inner(re, im, fwd_b)

    def filtered(got, f):
        re, im = got[:, :W], got[:, W:]
        tap_re, tap_im = spec[f, :, :W], spec[f, :, W:]
        re, im = re * tap_re - im * tap_im, re * tap_im + im * tap_re
        mid = inner(re, im, inv_b)
        re, im = rotate(mid[:, :W], mid[:, W:], -1.0)
        return parts(jnp.concatenate([re, im], axis=0), 0)

    sub = lax.broadcasted_iota(jnp.int32, (W, W), 1)

    def short(t):
        rows = []
        for b in range(N):
            total = jnp.zeros((N, W), BF16)
            for s in range(N):
                total = jnp.where(ids_row[s] == b, recv_sig[s, t], total)
            rows.append(total)
        stream = jnp.concatenate(rows, axis=0).astype(F32)
        before = jnp.concatenate([jnp.zeros((N, W), F32), stream[:-N]], axis=0)
        one = pltpu.roll(jnp.where(sub == W - 1, before, stream), 1, 1)
        two = pltpu.roll(jnp.where(sub >= W - 2, before, stream), 2, 1)
        tap = [column_of(short_filter[i : i + 1, t * W : (t + 1) * W]) for i in range(3)]
        blocks = lambda x: x.reshape(N, N, W)
        return (tap[0] * blocks(stream) + tap[1] * blocks(one) + tap[2] * blocks(two)).reshape(W, W)

    for i in (7, 11, 8, 5, 4, 9, 10):
        loads[i].wait()
    gain = [column_of(skip_gain[i : i + 1, :]) for i in range(2)]
    scaled = lambda g, x: (g * x.reshape(-1, N, W)).reshape(-1, W)
    spectrum = lambda f: forward(recv_tap[:, f].reshape(W, W))

    for k in FAR[::-1]:
        block_arrival(k).wait_recv()
    for s in range(N):
        ids_row[s] = jnp.broadcast_to(recv_blk[s].astype(F32), (N, W)).astype(BF16)
    for k in FAR[::-1]:
        third_arrival(0, k).wait_recv()
    value = short(0)
    ahead = forward(value)
    for k in FAR[::-1]:
        third_arrival(1, k).wait_recv()
    gate[...] = short(1)
    for k in range(1, chips):
        tap_arrival(k).wait_recv()
    spec[0] = spectrum(0)
    first = gate[...] * (dot(inv_a[...], filtered(ahead, 0)) + scaled(gain[0], value))
    passed[...] = scaled(gain[1], first)
    spec[1] = spectrum(1)
    ahead = filtered(forward(first), 1)
    for k in FAR[::-1]:
        third_arrival(2, k).wait_recv()
    gate[...] = short(2)

    def out_copy(k):
        peer = (me + k) % N
        return pltpu.make_async_remote_copy(
            src_ref=gated.at[peer],
            dst_ref=out.at[me],
            send_sem=out_send.at[peer],
            recv_sem=out_recv.at[me],
            device_id={"seq": peer},
        )

    def out_arrival(k):
        peer = (me + k) % N
        return pltpu.make_async_remote_copy(
            src_ref=gated.at[peer],
            dst_ref=out.at[peer],
            send_sem=out_send.at[peer],
            recv_sem=out_recv.at[peer],
            device_id={"seq": peer},
        )

    for g in (2, 1, 3, 0):
        group = (me // 4 + g) % 4
        at = pl.ds(pl.multiple_of(group * 64, 64), 64)
        rows = gate[at, :] * (dot(inv_a[at, :], ahead) + passed[at, :])
        gated[pl.ds(group * 4, 4)] = rows.astype(BF16).reshape(4, N, W)
        for i in range(4):
            peer = group * 4 + i

            @pl.when(peer != me)
            def _():
                out_copy((peer + N - me) % N).start()

    own = pltpu.make_async_copy(gated.at[me], out.at[me], keep_sem)
    own.start()

    @pl.when(column != 0)
    def _():
        tap_first().wait_send()

    each(N, lambda k: block_copy(k).wait_send())
    for part in range(3):
        each(N, lambda k: third_copy(part, k).wait_send())
    each(chips, lambda k: tap_copy(k).wait_send())
    each(N, lambda k: out_copy(k).wait_send())
    for k in FAR[::-1]:
        out_arrival(k).wait_recv()
    own.wait()


def body(n_batch, events, positions, length, filters, skip_gain, short_filter, in_proj, out_proj):
    tables = [jnp.asarray(table) for table in make_tables()]
    inputs = [
        length.reshape(1, 1),
        positions.reshape(1, W),
        events,
        filters,
        skip_gain,
        short_filter,
        in_proj,
        *tables,
    ]
    dma = lambda *shape: pltpu.SemaphoreType.DMA(shape)
    held = [pltpu.VMEM((W, 2, 128) if i == 3 else x.shape, x.dtype) for i, x in enumerate(inputs)]
    gated = pl.pallas_call(
        functools.partial(kernel, n_batch),
        out_shape=jax.ShapeDtypeStruct((N, N, W), BF16),
        in_specs=[pl.BlockSpec(memory_space=pl.ANY)] * INPUTS,
        out_specs=pl.BlockSpec(memory_space=pl.ANY),
        scratch_shapes=held
        + [
            pltpu.VMEM((N, 3, N, W), BF16),
            pltpu.VMEM((1, W), jnp.int32),
            pltpu.VMEM((2, N, W), BF16),
            pltpu.VMEM((N, N, W), BF16),
            pltpu.VMEM((W, W), F32),
            pltpu.VMEM((W, W), F32),
            pltpu.VMEM((N, N, W), BF16),
            pltpu.VMEM((N, 3, N, W), BF16),
            pltpu.VMEM((N, 1, W), jnp.int32),
            pltpu.VMEM((N, 2, N, W), BF16),
            pltpu.VMEM((2, W, 2 * W), F32),
            dma(INPUTS),
            dma(3, N),
            dma(3, N),
            dma(N),
            dma(N),
            dma(n_batch // 2),
            dma(n_batch // 2),
            pltpu.SemaphoreType.DMA,
            pltpu.SemaphoreType.DMA,
            pltpu.SemaphoreType.DMA,
            dma(N),
            dma(N),
        ],
        compiler_params=pltpu.CompilerParams(
            collective_id=0, has_side_effects=True, vmem_limit_bytes=63 * 1024 * 1024
        ),
    )(*inputs)
    return dot(gated.reshape(W, W), out_proj, ((0,), (0,))).astype(BF16)


def solution(mesh):
    return jax.shard_map(
        functools.partial(body, mesh.shape["batch"]),
        mesh=mesh,
        in_specs=(
            P(("batch", "seq"), None),
            P(("batch", "seq")),
            P("batch"),
            P("seq", None, None),
            P(),
            P(),
            P(),
            P(),
        ),
        out_specs=P(("batch", "seq"), None),
        check_vma=False,
    )
```

```python
import functools
import math

import jax
import jax.numpy as jnp
import ml_dtypes
import numpy as np
from jax import lax
from jax.experimental import pallas as pl
from jax.experimental.pallas import tpu as pltpu
from jax.sharding import PartitionSpec as P

N = 16
FAR = (8, 7, 9, 6, 10, 5, 11, 4, 12, 3, 13, 2, 14, 1, 15)
W = 256
POINTS = 2 * N * W
F32, BF16 = jnp.float32, jnp.bfloat16


def split(table):
    high = table.astype(ml_dtypes.bfloat16)
    low = (table - high.astype(np.float64)).astype(ml_dtypes.bfloat16)
    return high, low


@functools.cache
def make_tables():
    half = np.arange(N) + 0.5
    outer = 2 * np.pi * np.outer(half, np.arange(N)) / (2 * N)
    eye = np.eye(N)
    fwd_a = np.concatenate([np.kron(np.cos(outer), eye), np.kron(-np.sin(outer), eye)], 0)
    inv_a = np.concatenate([np.kron(np.cos(outer.T), eye), np.kron(-np.sin(outer.T), eye)], 1) * (2.0 / POINTS)
    inner = 2 * np.pi * (np.outer(np.arange(W), np.arange(W)) % W) / W
    cos, sin = np.cos(inner), np.sin(inner)
    fwd_b = np.block([[cos, -sin], [sin, cos]])
    inv_b = np.block([[cos, sin], [-sin, cos]])
    twist = 2 * np.pi * np.outer(half, np.arange(W)) / POINTS
    cat = lambda table, axis, order=(0, 0, 1): np.concatenate([split(table)[i] for i in order], axis)
    return (
        cat(fwd_a, 1),
        cat(fwd_b, 0, (0, 1)),
        cat(inv_b, 0, (0, 1)),
        cat(inv_a, 1),
        np.stack([np.cos(twist), np.sin(twist)]).astype(np.float32),
    )


def parts(x, axis):
    high = x.astype(BF16)
    low = (x - high.astype(F32)).astype(BF16)
    return jnp.concatenate([high, low, high], axis=axis)


def dot(a, b, dims=((1,), (0,))):
    return lax.dot_general(a, b, (dims, ((), ())), preferred_element_type=F32)


INPUTS = 12


def kernel(n_batch, *refs):
    outside, (out, *inside), rest = refs[:INPUTS], refs[INPUTS : 2 * INPUTS + 1], refs[2 * INPUTS + 1 :]
    length, positions, events, filters, skip_gain, short_filter, in_proj, *tables = inside
    fwd_a, fwd_b, inv_b, inv_a, twist = tables
    (
        thirds,
        block_row,
        taps,
        gated,
        gate,
        passed,
        ids_row,
        recv_sig,
        recv_blk,
        recv_tap,
        spec,
        load_sem,
        sig_send,
        sig_recv,
        blk_send,
        blk_recv,
        tap_send,
        tap_recv,
        own_send,
        own_recv,
        keep_sem,
        out_send,
        out_recv,
    ) = rest
    me = lax.axis_index("seq")
    lane = lax.axis_index("batch")
    column, core = lane // 2, lane % 2
    chips = n_batch // 2
    shift = (column + N // 2 * core) % N
    target = (me + shift) % N

    barrier = pltpu.get_barrier_semaphore()
    for k in FAR:
        pl.semaphore_signal(barrier, inc=1, device_id={"seq": (me + k) % N})
    loads = []
    for i, (src, dst) in enumerate(zip(outside, inside)):
        if i == 3:
            src = src.at[:, :, pl.ds(pl.multiple_of(target // 8 * 128, 128), 128)]
        loads.append(pltpu.make_async_copy(src, dst, load_sem.at[i]))
    for i in (1, 2, 6, 0, 3):
        loads[i].start()
    for k in range(1, chips):
        pl.semaphore_signal(barrier, inc=1, device_id={"batch": (lane + 2 * k) % n_batch})
    for i in (7, 11, 8, 5, 4, 9, 10):
        loads[i].start()

    for i in (1, 0, 2, 6):
        loads[i].wait()
    pos = positions[...]
    order = lax.broadcasted_iota(jnp.int32, (W, W), 0) == pos % W
    one_hot = order.astype(BF16)
    kept = jnp.where(pos < length[...], one_hot, jnp.zeros_like(one_hot))
    ids = jnp.broadcast_to((pos // W).astype(BF16), (N, W))
    block_row[...] = dot(ids, one_hot, ((1,), (1,)))[0:1].astype(jnp.int32)
    ordered = dot(kept, events[...]).astype(BF16)

    def project(t):
        projected = dot(ordered, in_proj[:, t * W : (t + 1) * W])
        thirds[:, t] = projected.T.astype(BF16).reshape(N, N, W)

    project(0)
    loads[3].wait()
    rows16 = lax.broadcasted_iota(jnp.int32, (N, W), 0)
    lanes16 = lax.broadcasted_iota(jnp.int32, (N, W), 1)
    pick = (lanes16[:, :128] == rows16[:, :128] + target % 8 * N).astype(BF16)
    for f in range(2):
        taps[f] = dot(pick, filters[:, f, :].astype(BF16), ((1,), (1,))).astype(BF16)
    pl.semaphore_wait(barrier, N - 1 + chips - 1)

    def tap_first():
        return pltpu.make_async_remote_copy(
            src_ref=taps,
            dst_ref=recv_tap.at[me],
            send_sem=own_send,
            recv_sem=own_recv,
            device_id={"seq": target},
        )

    slot = (me + N - shift) % N

    def block_copy(k):
        peer = (me + k) % N
        return pltpu.make_async_remote_copy(
            src_ref=block_row,
            dst_ref=recv_blk.at[me],
            send_sem=blk_send.at[peer],
            recv_sem=blk_recv.at[me],
            device_id={"seq": peer},
        )

    def block_arrival(k):
        peer = (me + k) % N
        return pltpu.make_async_remote_copy(
            src_ref=block_row,
            dst_ref=recv_blk.at[peer],
            send_sem=blk_send.at[peer],
            recv_sem=blk_recv.at[peer],
            device_id={"seq": peer},
        )

    def third_copy(part, k):
        peer = (me + k) % N
        return pltpu.make_async_remote_copy(
            src_ref=thirds.at[peer, part],
            dst_ref=recv_sig.at[me, part],
            send_sem=sig_send.at[part, peer],
            recv_sem=sig_recv.at[part, me],
            device_id={"seq": peer},
        )

    def third_arrival(part, k):
        peer = (me + k) % N
        return pltpu.make_async_remote_copy(
            src_ref=thirds.at[peer, part],
            dst_ref=recv_sig.at[peer, part],
            send_sem=sig_send.at[part, peer],
            recv_sem=sig_recv.at[part, peer],
            device_id={"seq": peer},
        )

    def each(count, act):
        def step(k, carry):
            act(k)
            return carry

        lax.fori_loop(1, count, step, 0)

    @pl.when(shift != 0)
    def _():
        tap_first().start()

    @pl.when(shift == 0)
    def _():
        recv_tap[me] = taps[...]

    for k in FAR:
        block_copy(k).start()
        third_copy(0, k).start()
    project(1)
    for k in FAR:
        third_copy(1, k).start()
    project(2)
    recv_blk[me] = block_row[...]
    recv_sig[me] = thirds[me]

    @pl.when(shift != 0)
    def _():
        pltpu.make_async_remote_copy(
            src_ref=taps,
            dst_ref=recv_tap.at[slot],
            send_sem=own_send,
            recv_sem=own_recv,
            device_id={"seq": target},
        ).wait_recv()

    def tap_copy(k):
        peer = (column + k) % chips
        return pltpu.make_async_remote_copy(
            src_ref=recv_tap.at[slot],
            dst_ref=recv_tap.at[slot],
            send_sem=tap_send.at[peer],
            recv_sem=tap_recv.at[column],
            device_id={"batch": peer * 2 + core},
        )

    def tap_arrival(k):
        peer = (column + k) % chips
        there = recv_tap.at[(me + N - (peer + N // 2 * core) % N) % N]
        return pltpu.make_async_remote_copy(
            src_ref=there,
            dst_ref=there,
            send_sem=tap_send.at[peer],
            recv_sem=tap_recv.at[peer],
            device_id={"batch": peer * 2 + core},
        )

    for k in range(1, chips):
        tap_copy(k).start()
    for k in FAR:
        third_copy(2, k).start()

    def column_of(row):
        return jnp.sum(jnp.where(lanes16 == rows16 + me * N, row, 0.0), axis=1, keepdims=True)[None]

    def rotate(re, im, sign):
        cos = twist[0][:, None, :]
        sin = twist[1][:, None, :] * sign
        re, im = re.reshape(N, N, W), im.reshape(N, N, W)
        return (re * cos + im * sin).reshape(W, W), (im * cos - re * sin).reshape(W, W)

    def inner(re, im, table):
        x = jnp.concatenate([re, im], axis=1).astype(BF16)
        return dot(jnp.concatenate([x, x], axis=1), table[...])

    def forward(signal):
        if signal.dtype == BF16:
            mid = dot(fwd_a[:, W:], jnp.concatenate([signal, signal], axis=0))
        else:
            mid = dot(fwd_a[...], parts(signal, 0))
        re, im = rotate(mid[:W], mid[W:], 1.0)
        return inner(re, im, fwd_b)

    def filtered(got, f):
        re, im = got[:, :W], got[:, W:]
        tap_re, tap_im = spec[f, :, :W], spec[f, :, W:]
        re, im = re * tap_re - im * tap_im, re * tap_im + im * tap_re
        mid = inner(re, im, inv_b)
        re, im = rotate(mid[:, :W], mid[:, W:], -1.0)
        return parts(jnp.concatenate([re, im], axis=0), 0)

    sub = lax.broadcasted_iota(jnp.int32, (W, W), 1)

    def short(t):
        rows = []
        for b in range(N):
            total = jnp.zeros((N, W), BF16)
            for s in range(N):
                total = jnp.where(ids_row[s] == b, recv_sig[s, t], total)
            rows.append(total)
        stream = jnp.concatenate(rows, axis=0).astype(F32)
        before = jnp.concatenate([jnp.zeros((N, W), F32), stream[:-N]], axis=0)
        one = pltpu.roll(jnp.where(sub == W - 1, before, stream), 1, 1)
        two = pltpu.roll(jnp.where(sub >= W - 2, before, stream), 2, 1)
        tap = [column_of(short_filter[i : i + 1, t * W : (t + 1) * W]) for i in range(3)]
        blocks = lambda x: x.reshape(N, N, W)
        return (tap[0] * blocks(stream) + tap[1] * blocks(one) + tap[2] * blocks(two)).reshape(W, W)

    for i in (7, 11, 8, 5, 4, 9, 10):
        loads[i].wait()
    gain = [column_of(skip_gain[i : i + 1, :]) for i in range(2)]
    scaled = lambda g, x: (g * x.reshape(-1, N, W)).reshape(-1, W)
    spectrum = lambda f: forward(recv_tap[:, f].reshape(W, W))

    for k in FAR[::-1]:
        block_arrival(k).wait_recv()
    for s in range(N):
        ids_row[s] = jnp.broadcast_to(recv_blk[s].astype(F32), (N, W)).astype(BF16)
    for k in FAR[::-1]:
        third_arrival(0, k).wait_recv()
    value = short(0)
    ahead = forward(value)
    for k in FAR[::-1]:
        third_arrival(1, k).wait_recv()
    gate[...] = short(1)
    for k in range(1, chips):
        tap_arrival(k).wait_recv()
    spec[0] = spectrum(0)
    first = gate[...] * (dot(inv_a[...], filtered(ahead, 0)) + scaled(gain[0], value))
    passed[...] = scaled(gain[1], first)
    spec[1] = spectrum(1)
    ahead = filtered(forward(first), 1)
    for k in FAR[::-1]:
        third_arrival(2, k).wait_recv()
    gate[...] = short(2)

    def out_copy(k):
        peer = (me + k) % N
        return pltpu.make_async_remote_copy(
            src_ref=gated.at[peer],
            dst_ref=out.at[me],
            send_sem=out_send.at[peer],
            recv_sem=out_recv.at[me],
            device_id={"seq": peer},
        )

    def out_arrival(k):
        peer = (me + k) % N
        return pltpu.make_async_remote_copy(
            src_ref=gated.at[peer],
            dst_ref=out.at[peer],
            send_sem=out_send.at[peer],
            recv_sem=out_recv.at[peer],
            device_id={"seq": peer},
        )

    gated[...] = (gate[...] * (dot(inv_a[...], ahead) + passed[...])).astype(BF16).reshape(N, N, W)
    for k in FAR:
        out_copy(k).start()
    own = pltpu.make_async_copy(gated.at[me], out.at[me], keep_sem)
    own.start()

    @pl.when(shift != 0)
    def _():
        tap_first().wait_send()

    each(N, lambda k: block_copy(k).wait_send())
    for part in range(3):
        each(N, lambda k: third_copy(part, k).wait_send())
    each(chips, lambda k: tap_copy(k).wait_send())
    each(N, lambda k: out_copy(k).wait_send())
    for k in FAR[::-1]:
        out_arrival(k).wait_recv()
    own.wait()


def body(n_batch, events, positions, length, filters, skip_gain, short_filter, in_proj, out_proj):
    tables = [jnp.asarray(table) for table in make_tables()]
    inputs = [
        length.reshape(1, 1),
        positions.reshape(1, W),
        events,
        filters,
        skip_gain,
        short_filter,
        in_proj,
        *tables,
    ]
    dma = lambda *shape: pltpu.SemaphoreType.DMA(shape)
    held = [pltpu.VMEM((W, 2, 128) if i == 3 else x.shape, x.dtype) for i, x in enumerate(inputs)]
    gated = pl.pallas_call(
        functools.partial(kernel, n_batch),
        out_shape=jax.ShapeDtypeStruct((N, N, W), BF16),
        in_specs=[pl.BlockSpec(memory_space=pl.ANY)] * INPUTS,
        out_specs=pl.BlockSpec(memory_space=pl.ANY),
        scratch_shapes=held
        + [
            pltpu.VMEM((N, 3, N, W), BF16),
            pltpu.VMEM((1, W), jnp.int32),
            pltpu.VMEM((2, N, W), BF16),
            pltpu.VMEM((N, N, W), BF16),
            pltpu.VMEM((W, W), F32),
            pltpu.VMEM((W, W), F32),
            pltpu.VMEM((N, N, W), BF16),
            pltpu.VMEM((N, 3, N, W), BF16),
            pltpu.VMEM((N, 1, W), jnp.int32),
            pltpu.VMEM((N, 2, N, W), BF16),
            pltpu.VMEM((2, W, 2 * W), F32),
            dma(INPUTS),
            dma(3, N),
            dma(3, N),
            dma(N),
            dma(N),
            dma(n_batch // 2),
            dma(n_batch // 2),
            pltpu.SemaphoreType.DMA,
            pltpu.SemaphoreType.DMA,
            pltpu.SemaphoreType.DMA,
            dma(N),
            dma(N),
        ],
        compiler_params=pltpu.CompilerParams(
            collective_id=0, has_side_effects=True, vmem_limit_bytes=63 * 1024 * 1024
        ),
    )(*inputs)
    return dot(gated.reshape(W, W), out_proj, ((0,), (0,))).astype(BF16)


def solution(mesh):
    return jax.shard_map(
        functools.partial(body, mesh.shape["batch"]),
        mesh=mesh,
        in_specs=(
            P(("batch", "seq"), None),
            P(("batch", "seq")),
            P("batch"),
            P("seq", None, None),
            P(),
            P(),
            P(),
            P(),
        ),
        out_specs=P(("batch", "seq"), None),
        check_vma=False,
    )
```

```python
import functools
import math

import jax
import jax.numpy as jnp
import ml_dtypes
import numpy as np
from jax import lax
from jax.experimental import pallas as pl
from jax.experimental.pallas import tpu as pltpu
from jax.sharding import PartitionSpec as P

N = 16
FAR = (8, 7, 9, 6, 10, 5, 11, 4, 12, 3, 13, 2, 14, 1, 15)
W = 256
POINTS = 2 * N * W
F32, BF16 = jnp.float32, jnp.bfloat16


def split(table):
    high = table.astype(ml_dtypes.bfloat16)
    low = (table - high.astype(np.float64)).astype(ml_dtypes.bfloat16)
    return high, low


@functools.cache
def make_tables():
    half = np.arange(N) + 0.5
    outer = 2 * np.pi * np.outer(half, np.arange(N)) / (2 * N)
    eye = np.eye(N)
    fwd_a = np.concatenate([np.kron(np.cos(outer), eye), np.kron(-np.sin(outer), eye)], 0)
    inv_a = np.concatenate([np.kron(np.cos(outer.T), eye), np.kron(-np.sin(outer.T), eye)], 1) * (2.0 / POINTS)
    inner = 2 * np.pi * (np.outer(np.arange(W), np.arange(W)) % W) / W
    cos, sin = np.cos(inner), np.sin(inner)
    fwd_b = np.block([[cos, -sin], [sin, cos]])
    inv_b = np.block([[cos, sin], [-sin, cos]])
    twist = 2 * np.pi * np.outer(half, np.arange(W)) / POINTS
    cat = lambda table, axis, order=(0, 0, 1): np.concatenate([split(table)[i] for i in order], axis)
    return (
        cat(fwd_a, 1),
        cat(fwd_b, 0, (0, 1)),
        cat(inv_b, 0, (0, 1)),
        cat(inv_a, 1),
        np.stack([np.cos(twist), np.sin(twist)]).astype(np.float32),
    )


def parts(x, axis):
    high = x.astype(BF16)
    low = (x - high.astype(F32)).astype(BF16)
    return jnp.concatenate([high, low, high], axis=axis)


def dot(a, b, dims=((1,), (0,))):
    return lax.dot_general(a, b, (dims, ((), ())), preferred_element_type=F32)


INPUTS = 12


def kernel(n_batch, *refs):
    outside, (out, side, *inside), rest = refs[:INPUTS], refs[INPUTS : 2 * INPUTS + 2], refs[2 * INPUTS + 2 :]
    length, positions, events, filters, skip_gain, short_filter, in_proj, *tables = inside
    fwd_a, fwd_b, inv_b, inv_a, twist = tables
    (
        thirds,
        block_row,
        taps,
        gated,
        gate,
        passed,
        ids_row,
        sent_rows,
        recv_rows,
        tail_rows,
        halo,
        recv_sig,
        recv_blk,
        recv_tap,
        spec,
        load_sem,
        sig_send,
        sig_recv,
        blk_send,
        blk_recv,
        tap_send,
        tap_recv,
        own_send,
        own_recv,
        keep_sem,
        side_sem,
        halo_send,
        halo_recv,
        out_send,
        out_recv,
    ) = rest
    me = lax.axis_index("seq")
    lane = lax.axis_index("batch")
    column, core = lane // 2, lane % 2
    chips = n_batch // 2
    shift = (column + N // 2 * core) % N
    target = (me + shift) % N

    barrier = pltpu.get_barrier_semaphore()
    for k in FAR:
        pl.semaphore_signal(barrier, inc=1, device_id={"seq": (me + k) % N})
    loads = []
    for i, (src, dst) in enumerate(zip(outside, inside)):
        if i == 3:
            src = src.at[:, :, pl.ds(pl.multiple_of(target // 8 * 128, 128), 128)]
        loads.append(pltpu.make_async_copy(src, dst, load_sem.at[i]))
    for i in (1, 2, 6, 0, 3):
        loads[i].start()
    for k in range(1, chips):
        pl.semaphore_signal(barrier, inc=1, device_id={"batch": (lane + 2 * k) % n_batch})
    for i in (7, 11, 8, 5, 4, 9, 10):
        loads[i].start()

    for i in (1, 0, 2, 6):
        loads[i].wait()
    pos = positions[...]
    order = lax.broadcasted_iota(jnp.int32, (W, W), 0) == pos % W
    one_hot = order.astype(BF16)
    kept = jnp.where(pos < length[...], one_hot, jnp.zeros_like(one_hot))
    ids = jnp.broadcast_to((pos // W).astype(BF16), (N, W))
    block_row[...] = dot(ids, one_hot, ((1,), (1,)))[0:1].astype(jnp.int32)
    ordered = dot(kept, events[...]).astype(BF16)

    def project(t):
        projected = dot(ordered, in_proj[:, t * W : (t + 1) * W])
        thirds[:, t] = projected.T.astype(BF16).reshape(N, N, W)

    project(0)
    loads[3].wait()
    rows16 = lax.broadcasted_iota(jnp.int32, (N, W), 0)
    lanes16 = lax.broadcasted_iota(jnp.int32, (N, W), 1)
    pick = (lanes16[:, :128] == rows16[:, :128] + target % 8 * N).astype(BF16)
    for f in range(2):
        taps[f] = dot(pick, filters[:, f, :].astype(BF16), ((1,), (1,))).astype(BF16)
    pl.semaphore_wait(barrier, N - 1 + chips - 1)

    def tap_first():
        return pltpu.make_async_remote_copy(
            src_ref=taps,
            dst_ref=recv_tap.at[me],
            send_sem=own_send,
            recv_sem=own_recv,
            device_id={"seq": target},
        )

    slot = (me + N - shift) % N

    def block_copy(k):
        peer = (me + k) % N
        return pltpu.make_async_remote_copy(
            src_ref=block_row,
            dst_ref=recv_blk.at[me],
            send_sem=blk_send.at[peer],
            recv_sem=blk_recv.at[me],
            device_id={"seq": peer},
        )

    def block_arrival(k):
        peer = (me + k) % N
        return pltpu.make_async_remote_copy(
            src_ref=block_row,
            dst_ref=recv_blk.at[peer],
            send_sem=blk_send.at[peer],
            recv_sem=blk_recv.at[peer],
            device_id={"seq": peer},
        )

    def third_copy(part, k):
        peer = (me + k) % N
        return pltpu.make_async_remote_copy(
            src_ref=thirds.at[peer, part],
            dst_ref=recv_sig.at[me, part],
            send_sem=sig_send.at[part, peer],
            recv_sem=sig_recv.at[part, me],
            device_id={"seq": peer},
        )

    def third_arrival(part, k):
        peer = (me + k) % N
        return pltpu.make_async_remote_copy(
            src_ref=thirds.at[peer, part],
            dst_ref=recv_sig.at[peer, part],
            send_sem=sig_send.at[part, peer],
            recv_sem=sig_recv.at[part, peer],
            device_id={"seq": peer},
        )

    def each(count, act):
        def step(k, carry):
            act(k)
            return carry

        lax.fori_loop(1, count, step, 0)

    @pl.when(shift != 0)
    def _():
        tap_first().start()

    @pl.when(shift == 0)
    def _():
        recv_tap[me] = taps[...]

    for k in FAR:
        block_copy(k).start()
        third_copy(0, k).start()
    project(1)
    for k in FAR:
        third_copy(1, k).start()
    by_block = lax.broadcasted_iota(jnp.int32, (W, W), 0) == pos // W * N + pos % N
    by_block = jnp.where(by_block & (pos < length[...]), 1.0, 0.0).astype(BF16)
    rows = dot(by_block, events[...]).astype(BF16)
    sent_rows[...] = dot(rows, in_proj[:, 2 * W :]).astype(BF16).reshape(N, N, W)
    recv_rows[me] = sent_rows[me]
    recv_blk[me] = block_row[...]
    recv_sig[me] = thirds[me]

    def rows_copy(k):
        peer = (me + k) % N
        return pltpu.make_async_remote_copy(
            src_ref=sent_rows.at[peer],
            dst_ref=recv_rows.at[me],
            send_sem=sig_send.at[2, peer],
            recv_sem=sig_recv.at[2, me],
            device_id={"seq": peer},
        )

    def rows_arrival(k):
        peer = (me + k) % N
        return pltpu.make_async_remote_copy(
            src_ref=sent_rows.at[peer],
            dst_ref=recv_rows.at[peer],
            send_sem=sig_send.at[2, peer],
            recv_sem=sig_recv.at[2, peer],
            device_id={"seq": peer},
        )

    def halo_copy(step):
        return pltpu.make_async_remote_copy(
            src_ref=tail_rows,
            dst_ref=halo,
            send_sem=halo_send,
            recv_sem=halo_recv,
            device_id={"seq": (me + step) % N},
        )

    @pl.when(shift != 0)
    def _():
        pltpu.make_async_remote_copy(
            src_ref=taps,
            dst_ref=recv_tap.at[slot],
            send_sem=own_send,
            recv_sem=own_recv,
            device_id={"seq": target},
        ).wait_recv()

    def tap_copy(k):
        peer = (column + k) % chips
        return pltpu.make_async_remote_copy(
            src_ref=recv_tap.at[slot],
            dst_ref=recv_tap.at[slot],
            send_sem=tap_send.at[peer],
            recv_sem=tap_recv.at[column],
            device_id={"batch": peer * 2 + core},
        )

    def tap_arrival(k):
        peer = (column + k) % chips
        there = recv_tap.at[(me + N - (peer + N // 2 * core) % N) % N]
        return pltpu.make_async_remote_copy(
            src_ref=there,
            dst_ref=there,
            send_sem=tap_send.at[peer],
            recv_sem=tap_recv.at[peer],
            device_id={"batch": peer * 2 + core},
        )

    for k in range(1, chips):
        tap_copy(k).start()
    for k in FAR:
        rows_copy(k).start()

    def column_of(row):
        return jnp.sum(jnp.where(lanes16 == rows16 + me * N, row, 0.0), axis=1, keepdims=True)[None]

    def rotate(re, im, sign):
        cos = twist[0][:, None, :]
        sin = twist[1][:, None, :] * sign
        re, im = re.reshape(N, N, W), im.reshape(N, N, W)
        return (re * cos + im * sin).reshape(W, W), (im * cos - re * sin).reshape(W, W)

    def inner(re, im, table):
        x = jnp.concatenate([re, im], axis=1).astype(BF16)
        return dot(jnp.concatenate([x, x], axis=1), table[...])

    def forward(signal):
        if signal.dtype == BF16:
            mid = dot(fwd_a[:, W:], jnp.concatenate([signal, signal], axis=0))
        else:
            mid = dot(fwd_a[...], parts(signal, 0))
        re, im = rotate(mid[:W], mid[W:], 1.0)
        return inner(re, im, fwd_b)

    def filtered(got, f):
        re, im = got[:, :W], got[:, W:]
        tap_re, tap_im = spec[f, :, :W], spec[f, :, W:]
        re, im = re * tap_re - im * tap_im, re * tap_im + im * tap_re
        mid = inner(re, im, inv_b)
        re, im = rotate(mid[:, :W], mid[:, W:], -1.0)
        return parts(jnp.concatenate([re, im], axis=0), 0)

    sub = lax.broadcasted_iota(jnp.int32, (W, W), 1)

    def short(t):
        rows = []
        for b in range(N):
            total = jnp.zeros((N, W), BF16)
            for s in range(N):
                total = jnp.where(ids_row[s] == b, recv_sig[s, t], total)
            rows.append(total)
        stream = jnp.concatenate(rows, axis=0).astype(F32)
        before = jnp.concatenate([jnp.zeros((N, W), F32), stream[:-N]], axis=0)
        one = pltpu.roll(jnp.where(sub == W - 1, before, stream), 1, 1)
        two = pltpu.roll(jnp.where(sub >= W - 2, before, stream), 2, 1)
        tap = [column_of(short_filter[i : i + 1, t * W : (t + 1) * W]) for i in range(3)]
        blocks = lambda x: x.reshape(N, N, W)
        return (tap[0] * blocks(stream) + tap[1] * blocks(one) + tap[2] * blocks(two)).reshape(W, W)

    for i in (7, 11, 8, 5, 4, 9, 10):
        loads[i].wait()
    gain = [column_of(skip_gain[i : i + 1, :]) for i in range(2)]
    scaled = lambda g, x: (g * x.reshape(-1, N, W)).reshape(-1, W)
    spectrum = lambda f: forward(recv_tap[:, f].reshape(W, W))

    for k in FAR[::-1]:
        block_arrival(k).wait_recv()
    for s in range(N):
        ids_row[s] = jnp.broadcast_to(recv_blk[s].astype(F32), (N, W)).astype(BF16)
    for k in FAR[::-1]:
        third_arrival(0, k).wait_recv()
    value = short(0)
    ahead = forward(value)
    for k in FAR[::-1]:
        third_arrival(1, k).wait_recv()
    gate[...] = short(1)
    for k in range(1, chips):
        tap_arrival(k).wait_recv()
    spec[0] = spectrum(0)
    first = gate[...] * (dot(inv_a[...], filtered(ahead, 0)) + scaled(gain[0], value))
    passed[...] = scaled(gain[1], first)
    spec[1] = spectrum(1)
    ahead = filtered(forward(first), 1)
    def out_copy(k):
        peer = (me + k) % N
        return pltpu.make_async_remote_copy(
            src_ref=gated.at[peer],
            dst_ref=out.at[me],
            send_sem=out_send.at[peer],
            recv_sem=out_recv.at[me],
            device_id={"seq": peer},
        )

    def out_arrival(k):
        peer = (me + k) % N
        return pltpu.make_async_remote_copy(
            src_ref=gated.at[peer],
            dst_ref=out.at[peer],
            send_sem=out_send.at[peer],
            recv_sem=out_recv.at[peer],
            device_id={"seq": peer},
        )

    gated[...] = (dot(inv_a[...], ahead) + passed[...]).astype(BF16).reshape(N, N, W)
    for k in FAR:
        out_copy(k).start()
    own = pltpu.make_async_copy(gated.at[me], out.at[me], keep_sem)
    own.start()

    up = lax.broadcasted_iota(jnp.int32, (W, W), 0)
    place = (ids_row[...].reshape(W, W).astype(F32) == me.astype(F32)) & (up % N == sub % N)
    for k in FAR[::-1]:
        rows_arrival(k).wait_recv()
    stream = dot(jnp.where(place, 1.0, 0.0).astype(BF16), recv_rows[...].reshape(W, W), ((0,), (0,)))
    tail_rows[...] = stream[W - N :].astype(BF16)

    @pl.when(me < N - 1)
    def _():
        halo_copy(1).start()

    @pl.when(me == 0)
    def _():
        halo[...] = jnp.zeros_like(halo)

    @pl.when(me > 0)
    def _():
        halo_copy(N - 1).wait_recv()

    edge = halo[...].astype(F32)
    one = jnp.where(up == 0, edge[N - 1 :], pltpu.roll(stream, 1, 0))
    two = jnp.where(up == 0, edge[N - 2 : N - 1], jnp.where(up == 1, edge[N - 1 :], pltpu.roll(stream, 2, 0)))
    tap = [short_filter[i : i + 1, 2 * W :] for i in range(3)]
    gate[...] = (tap[0] * stream + tap[1] * one + tap[2] * two).T
    aside = pltpu.make_async_copy(gate, side, side_sem)
    aside.start()

    @pl.when(shift != 0)
    def _():
        tap_first().wait_send()

    each(N, lambda k: block_copy(k).wait_send())
    for part in range(2):
        each(N, lambda k: third_copy(part, k).wait_send())
    each(N, lambda k: rows_copy(k).wait_send())

    @pl.when(me < N - 1)
    def _():
        halo_copy(1).wait_send()

    each(chips, lambda k: tap_copy(k).wait_send())
    each(N, lambda k: out_copy(k).wait_send())
    for k in FAR[::-1]:
        out_arrival(k).wait_recv()
    own.wait()
    aside.wait()


def body(n_batch, events, positions, length, filters, skip_gain, short_filter, in_proj, out_proj):
    tables = [jnp.asarray(table) for table in make_tables()]
    inputs = [
        length.reshape(1, 1),
        positions.reshape(1, W),
        events,
        filters,
        skip_gain,
        short_filter,
        in_proj,
        *tables,
    ]
    dma = lambda *shape: pltpu.SemaphoreType.DMA(shape)
    held = [pltpu.VMEM((W, 2, 128) if i == 3 else x.shape, x.dtype) for i, x in enumerate(inputs)]
    second, gate = pl.pallas_call(
        functools.partial(kernel, n_batch),
        out_shape=(jax.ShapeDtypeStruct((N, N, W), BF16), jax.ShapeDtypeStruct((W, W), F32)),
        in_specs=[pl.BlockSpec(memory_space=pl.ANY)] * INPUTS,
        out_specs=(pl.BlockSpec(memory_space=pl.ANY),) * 2,
        scratch_shapes=held
        + [
            pltpu.VMEM((N, 2, N, W), BF16),
            pltpu.VMEM((1, W), jnp.int32),
            pltpu.VMEM((2, N, W), BF16),
            pltpu.VMEM((N, N, W), BF16),
            pltpu.VMEM((W, W), F32),
            pltpu.VMEM((W, W), F32),
            pltpu.VMEM((N, N, W), BF16),
            pltpu.VMEM((N, N, W), BF16),
            pltpu.VMEM((N, N, W), BF16),
            pltpu.VMEM((N, W), BF16),
            pltpu.VMEM((N, W), BF16),
            pltpu.VMEM((N, 2, N, W), BF16),
            pltpu.VMEM((N, 1, W), jnp.int32),
            pltpu.VMEM((N, 2, N, W), BF16),
            pltpu.VMEM((2, W, 2 * W), F32),
            dma(INPUTS),
            dma(3, N),
            dma(3, N),
            dma(N),
            dma(N),
            dma(n_batch // 2),
            dma(n_batch // 2),
            pltpu.SemaphoreType.DMA,
            pltpu.SemaphoreType.DMA,
            pltpu.SemaphoreType.DMA,
            pltpu.SemaphoreType.DMA,
            pltpu.SemaphoreType.DMA,
            pltpu.SemaphoreType.DMA,
            dma(N),
            dma(N),
        ],
        compiler_params=pltpu.CompilerParams(
            collective_id=0, has_side_effects=True, vmem_limit_bytes=63 * 1024 * 1024
        ),
    )(*inputs)
    gated = (gate * second.reshape(W, W).astype(F32)).astype(BF16)
    return dot(gated, out_proj, ((0,), (0,))).astype(BF16)


def solution(mesh):
    return jax.shard_map(
        functools.partial(body, mesh.shape["batch"]),
        mesh=mesh,
        in_specs=(
            P(("batch", "seq"), None),
            P(("batch", "seq")),
            P("batch"),
            P("seq", None, None),
            P(),
            P(),
            P(),
            P(),
        ),
        out_specs=P(("batch", "seq"), None),
        check_vma=False,
    )
```

```python
import functools
import math

import jax
import jax.numpy as jnp
import ml_dtypes
import numpy as np
from jax import lax
from jax.experimental import pallas as pl
from jax.experimental.pallas import tpu as pltpu
from jax.sharding import PartitionSpec as P

N = 16
FAR = (8, 7, 9, 6, 10, 5, 11, 4, 12, 3, 13, 2, 14, 1, 15)
W = 256
POINTS = 2 * N * W
F32, BF16 = jnp.float32, jnp.bfloat16


def split(table):
    high = table.astype(ml_dtypes.bfloat16)
    low = (table - high.astype(np.float64)).astype(ml_dtypes.bfloat16)
    return high, low


@functools.cache
def make_tables():
    half = np.arange(N) + 0.5
    outer = 2 * np.pi * np.outer(half, np.arange(N)) / (2 * N)
    eye = np.eye(N)
    fwd_a = np.concatenate([np.kron(np.cos(outer), eye), np.kron(-np.sin(outer), eye)], 0)
    inv_a = np.concatenate([np.kron(np.cos(outer.T), eye), np.kron(-np.sin(outer.T), eye)], 1) * (2.0 / POINTS)
    inner = 2 * np.pi * (np.outer(np.arange(W), np.arange(W)) % W) / W
    cos, sin = np.cos(inner), np.sin(inner)
    fwd_b = np.block([[cos, -sin], [sin, cos]])
    inv_b = np.block([[cos, sin], [-sin, cos]])
    twist = 2 * np.pi * np.outer(half, np.arange(W)) / POINTS
    cat = lambda table, axis, order=(0, 0, 1): np.concatenate([split(table)[i] for i in order], axis)
    return (
        cat(fwd_a, 1),
        cat(fwd_b, 0, (0, 1)),
        cat(inv_b, 0, (0, 1)),
        cat(inv_a, 1),
        np.stack([np.cos(twist), np.sin(twist)]).astype(np.float32),
    )


def parts(x, axis):
    high = x.astype(BF16)
    low = (x - high.astype(F32)).astype(BF16)
    return jnp.concatenate([high, low, high], axis=axis)


def dot(a, b, dims=((1,), (0,))):
    return lax.dot_general(a, b, (dims, ((), ())), preferred_element_type=F32)


INPUTS = 12


def kernel(n_batch, *refs):
    outside, (out, side, *inside), rest = refs[:INPUTS], refs[INPUTS : 2 * INPUTS + 2], refs[2 * INPUTS + 2 :]
    length, positions, events, filters, skip_gain, short_filter, in_proj, *tables = inside
    fwd_a, fwd_b, inv_b, inv_a, twist = tables
    (
        thirds,
        block_row,
        taps,
        gated,
        gate,
        passed,
        ids_row,
        sent_rows,
        recv_rows,
        tail_rows,
        halo,
        recv_sig,
        recv_blk,
        recv_tap,
        spec,
        load_sem,
        sig_send,
        sig_recv,
        blk_send,
        blk_recv,
        tap_send,
        tap_recv,
        own_send,
        own_recv,
        keep_sem,
        side_sem,
        halo_send,
        halo_recv,
        out_send,
        out_recv,
    ) = rest
    me = lax.axis_index("seq")
    lane = lax.axis_index("batch")
    column, core = lane // 2, lane % 2
    chips = n_batch // 2
    side_len = math.isqrt(chips)
    plane = [(dy, dx) for dy in range(side_len) for dx in range(side_len) if dy or dx]
    shift = (column + N // 2 * core) % N
    target = (me + shift) % N

    barrier = pltpu.get_barrier_semaphore()

    def chip_at(dy, dx):
        return (column // side_len + dy) % side_len * side_len + (column + dx) % side_len

    hops = [(min(k, N - k), k) for k in FAR]
    hops += [(min(dy, side_len - dy) + min(dx, side_len - dx), (dy, dx)) for dy, dx in plane]
    hops.sort(key=lambda item: -item[0])

    def greet(some):
        for _, to in some:
            if isinstance(to, tuple):
                peer = {"batch": chip_at(*to) * 2 + core}
            else:
                peer = {"seq": (me + to) % N}
            pl.semaphore_signal(barrier, inc=1, device_id=peer)

    greet(hops[: len(hops) // 2])
    loads = []
    for i, (src, dst) in enumerate(zip(outside, inside)):
        if i == 3:
            src = src.at[:, :, pl.ds(pl.multiple_of(target // 8 * 128, 128), 128)]
        loads.append(pltpu.make_async_copy(src, dst, load_sem.at[i]))
    for i in (1, 2, 6, 0, 3):
        loads[i].start()
    greet(hops[len(hops) // 2 :])
    for i in (7, 11, 8, 5, 4, 9, 10):
        loads[i].start()

    for i in (1, 0, 2, 6):
        loads[i].wait()
    pos = positions[...]
    order = lax.broadcasted_iota(jnp.int32, (W, W), 0) == pos % W
    one_hot = order.astype(BF16)
    kept = jnp.where(pos < length[...], one_hot, jnp.zeros_like(one_hot))
    ids = jnp.broadcast_to((pos // W).astype(BF16), (N, W))
    block_row[...] = dot(ids, one_hot, ((1,), (1,)))[0:1].astype(jnp.int32)
    ordered = dot(kept, events[...]).astype(BF16)

    def project(t):
        projected = dot(ordered, in_proj[:, t * W : (t + 1) * W])
        thirds[:, t] = projected.T.astype(BF16).reshape(N, N, W)

    project(0)
    loads[3].wait()
    rows16 = lax.broadcasted_iota(jnp.int32, (N, W), 0)
    lanes16 = lax.broadcasted_iota(jnp.int32, (N, W), 1)
    pick = (lanes16[:, :128] == rows16[:, :128] + target % 8 * N).astype(BF16)
    for f in range(2):
        taps[f] = dot(pick, filters[:, f, :].astype(BF16), ((1,), (1,))).astype(BF16)
    pl.semaphore_wait(barrier, N - 1 + chips - 1)

    def tap_first():
        return pltpu.make_async_remote_copy(
            src_ref=taps,
            dst_ref=recv_tap.at[me],
            send_sem=own_send,
            recv_sem=own_recv,
            device_id={"seq": target},
        )

    slot = (me + N - shift) % N

    def block_copy(k):
        peer = (me + k) % N
        return pltpu.make_async_remote_copy(
            src_ref=block_row,
            dst_ref=recv_blk.at[me],
            send_sem=blk_send.at[peer],
            recv_sem=blk_recv.at[me],
            device_id={"seq": peer},
        )

    def block_arrival(k):
        peer = (me + k) % N
        return pltpu.make_async_remote_copy(
            src_ref=block_row,
            dst_ref=recv_blk.at[peer],
            send_sem=blk_send.at[peer],
            recv_sem=blk_recv.at[peer],
            device_id={"seq": peer},
        )

    def third_copy(part, k):
        peer = (me + k) % N
        return pltpu.make_async_remote_copy(
            src_ref=thirds.at[peer, part],
            dst_ref=recv_sig.at[me, part],
            send_sem=sig_send.at[part, peer],
            recv_sem=sig_recv.at[part, me],
            device_id={"seq": peer},
        )

    def third_arrival(part, k):
        peer = (me + k) % N
        return pltpu.make_async_remote_copy(
            src_ref=thirds.at[peer, part],
            dst_ref=recv_sig.at[peer, part],
            send_sem=sig_send.at[part, peer],
            recv_sem=sig_recv.at[part, peer],
            device_id={"seq": peer},
        )

    def each(count, act):
        def step(k, carry):
            act(k)
            return carry

        lax.fori_loop(1, count, step, 0)

    @pl.when(shift != 0)
    def _():
        tap_first().start()

    @pl.when(shift == 0)
    def _():
        recv_tap[me] = taps[...]

    for k in FAR:
        block_copy(k).start()
        third_copy(0, k).start()
    project(1)
    for k in FAR:
        third_copy(1, k).start()
    by_block = lax.broadcasted_iota(jnp.int32, (W, W), 0) == pos // W * N + pos % N
    by_block = jnp.where(by_block & (pos < length[...]), 1.0, 0.0).astype(BF16)
    rows = dot(by_block, events[...]).astype(BF16)
    sent_rows[...] = dot(rows, in_proj[:, 2 * W :]).astype(BF16).reshape(N, N, W)
    recv_rows[me] = sent_rows[me]
    recv_blk[me] = block_row[...]
    recv_sig[me] = thirds[me]

    def rows_copy(k):
        peer = (me + k) % N
        return pltpu.make_async_remote_copy(
            src_ref=sent_rows.at[peer],
            dst_ref=recv_rows.at[me],
            send_sem=sig_send.at[2, peer],
            recv_sem=sig_recv.at[2, me],
            device_id={"seq": peer},
        )

    def rows_arrival(k):
        peer = (me + k) % N
        return pltpu.make_async_remote_copy(
            src_ref=sent_rows.at[peer],
            dst_ref=recv_rows.at[peer],
            send_sem=sig_send.at[2, peer],
            recv_sem=sig_recv.at[2, peer],
            device_id={"seq": peer},
        )

    def halo_copy(step):
        return pltpu.make_async_remote_copy(
            src_ref=tail_rows,
            dst_ref=halo,
            send_sem=halo_send,
            recv_sem=halo_recv,
            device_id={"seq": (me + step) % N},
        )

    @pl.when(shift != 0)
    def _():
        pltpu.make_async_remote_copy(
            src_ref=taps,
            dst_ref=recv_tap.at[slot],
            send_sem=own_send,
            recv_sem=own_recv,
            device_id={"seq": target},
        ).wait_recv()

    def tap_copy(peer):
        return pltpu.make_async_remote_copy(
            src_ref=recv_tap.at[slot],
            dst_ref=recv_tap.at[slot],
            send_sem=tap_send.at[peer],
            recv_sem=tap_recv.at[column],
            device_id={"batch": peer * 2 + core},
        )

    def tap_arrival(k):
        peer = (column + k) % chips
        there = recv_tap.at[(me + N - (peer + N // 2 * core) % N) % N]
        return pltpu.make_async_remote_copy(
            src_ref=there,
            dst_ref=there,
            send_sem=tap_send.at[peer],
            recv_sem=tap_recv.at[peer],
            device_id={"batch": peer * 2 + core},
        )

    for _, to in hops:
        if isinstance(to, tuple):
            tap_copy(chip_at(*to)).start()
    for k in FAR:
        rows_copy(k).start()

    def column_of(row):
        return jnp.sum(jnp.where(lanes16 == rows16 + me * N, row, 0.0), axis=1, keepdims=True)[None]

    def rotate(re, im, sign):
        cos = twist[0][:, None, :]
        sin = twist[1][:, None, :] * sign
        re, im = re.reshape(N, N, W), im.reshape(N, N, W)
        return (re * cos + im * sin).reshape(W, W), (im * cos - re * sin).reshape(W, W)

    def inner(re, im, table):
        x = jnp.concatenate([re, im], axis=1).astype(BF16)
        return dot(jnp.concatenate([x, x], axis=1), table[...])

    def forward(signal):
        if signal.dtype == BF16:
            mid = dot(fwd_a[:, W:], jnp.concatenate([signal, signal], axis=0))
        else:
            mid = dot(fwd_a[...], parts(signal, 0))
        re, im = rotate(mid[:W], mid[W:], 1.0)
        return inner(re, im, fwd_b)

    def filtered(got, f):
        re, im = got[:, :W], got[:, W:]
        tap_re, tap_im = spec[f, :, :W], spec[f, :, W:]
        re, im = re * tap_re - im * tap_im, re * tap_im + im * tap_re
        mid = inner(re, im, inv_b)
        re, im = rotate(mid[:, :W], mid[:, W:], -1.0)
        return parts(jnp.concatenate([re, im], axis=0), 0)

    sub = lax.broadcasted_iota(jnp.int32, (W, W), 1)

    def short(t):
        rows = []
        for b in range(N):
            total = jnp.zeros((N, W), BF16)
            for s in range(N):
                total = jnp.where(ids_row[s] == b, recv_sig[s, t], total)
            rows.append(total)
        stream = jnp.concatenate(rows, axis=0).astype(F32)
        before = jnp.concatenate([jnp.zeros((N, W), F32), stream[:-N]], axis=0)
        one = pltpu.roll(jnp.where(sub == W - 1, before, stream), 1, 1)
        two = pltpu.roll(jnp.where(sub >= W - 2, before, stream), 2, 1)
        tap = [column_of(short_filter[i : i + 1, t * W : (t + 1) * W]) for i in range(3)]
        blocks = lambda x: x.reshape(N, N, W)
        return (tap[0] * blocks(stream) + tap[1] * blocks(one) + tap[2] * blocks(two)).reshape(W, W)

    for i in (7, 11, 8, 5, 4, 9, 10):
        loads[i].wait()
    gain = [column_of(skip_gain[i : i + 1, :]) for i in range(2)]
    scaled = lambda g, x: (g * x.reshape(-1, N, W)).reshape(-1, W)
    spectrum = lambda f: forward(recv_tap[:, f].reshape(W, W))

    for k in FAR[::-1]:
        block_arrival(k).wait_recv()
    for s in range(N):
        ids_row[s] = jnp.broadcast_to(recv_blk[s].astype(F32), (N, W)).astype(BF16)
    for k in FAR[::-1]:
        third_arrival(0, k).wait_recv()
    value = short(0)
    ahead = forward(value)
    for k in FAR[::-1]:
        third_arrival(1, k).wait_recv()
    gate[...] = short(1)
    for k in range(1, chips):
        tap_arrival(k).wait_recv()
    spec[0] = spectrum(0)
    first = gate[...] * (dot(inv_a[...], filtered(ahead, 0)) + scaled(gain[0], value))
    passed[...] = scaled(gain[1], first)
    spec[1] = spectrum(1)
    ahead = filtered(forward(first), 1)
    def out_copy(k):
        peer = (me + k) % N
        return pltpu.make_async_remote_copy(
            src_ref=gated.at[peer],
            dst_ref=out.at[me],
            send_sem=out_send.at[peer],
            recv_sem=out_recv.at[me],
            device_id={"seq": peer},
        )

    def out_arrival(k):
        peer = (me + k) % N
        return pltpu.make_async_remote_copy(
            src_ref=gated.at[peer],
            dst_ref=out.at[peer],
            send_sem=out_send.at[peer],
            recv_sem=out_recv.at[peer],
            device_id={"seq": peer},
        )

    gated[...] = (dot(inv_a[...], ahead) + passed[...]).astype(BF16).reshape(N, N, W)
    for k in FAR:
        out_copy(k).start()
    own = pltpu.make_async_copy(gated.at[me], out.at[me], keep_sem)
    own.start()

    up = lax.broadcasted_iota(jnp.int32, (W, W), 0)
    place = (ids_row[...].reshape(W, W).astype(F32) == me.astype(F32)) & (up % N == sub % N)
    for k in FAR[::-1]:
        rows_arrival(k).wait_recv()
    stream = dot(jnp.where(place, 1.0, 0.0).astype(BF16), recv_rows[...].reshape(W, W), ((0,), (0,)))
    tail_rows[...] = stream[W - N :].astype(BF16)

    @pl.when(me < N - 1)
    def _():
        halo_copy(1).start()

    @pl.when(me == 0)
    def _():
        halo[...] = jnp.zeros_like(halo)

    @pl.when(me > 0)
    def _():
        halo_copy(N - 1).wait_recv()

    edge = halo[...].astype(F32)
    one = jnp.where(up == 0, edge[N - 1 :], pltpu.roll(stream, 1, 0))
    two = jnp.where(up == 0, edge[N - 2 : N - 1], jnp.where(up == 1, edge[N - 1 :], pltpu.roll(stream, 2, 0)))
    tap = [short_filter[i : i + 1, 2 * W :] for i in range(3)]
    gate[...] = (tap[0] * stream + tap[1] * one + tap[2] * two).T
    aside = pltpu.make_async_copy(gate, side, side_sem)
    aside.start()

    @pl.when(shift != 0)
    def _():
        tap_first().wait_send()

    each(N, lambda k: block_copy(k).wait_send())
    for part in range(2):
        each(N, lambda k: third_copy(part, k).wait_send())
    each(N, lambda k: rows_copy(k).wait_send())

    @pl.when(me < N - 1)
    def _():
        halo_copy(1).wait_send()

    each(chips, lambda k: tap_copy((column + k) % chips).wait_send())
    each(N, lambda k: out_copy(k).wait_send())
    for k in FAR[::-1]:
        out_arrival(k).wait_recv()
    own.wait()
    aside.wait()


def body(n_batch, events, positions, length, filters, skip_gain, short_filter, in_proj, out_proj):
    tables = [jnp.asarray(table) for table in make_tables()]
    inputs = [
        length.reshape(1, 1),
        positions.reshape(1, W),
        events,
        filters,
        skip_gain,
        short_filter,
        in_proj,
        *tables,
    ]
    dma = lambda *shape: pltpu.SemaphoreType.DMA(shape)
    held = [pltpu.VMEM((W, 2, 128) if i == 3 else x.shape, x.dtype) for i, x in enumerate(inputs)]
    second, gate = pl.pallas_call(
        functools.partial(kernel, n_batch),
        out_shape=(jax.ShapeDtypeStruct((N, N, W), BF16), jax.ShapeDtypeStruct((W, W), F32)),
        in_specs=[pl.BlockSpec(memory_space=pl.ANY)] * INPUTS,
        out_specs=(pl.BlockSpec(memory_space=pl.ANY),) * 2,
        scratch_shapes=held
        + [
            pltpu.VMEM((N, 2, N, W), BF16),
            pltpu.VMEM((1, W), jnp.int32),
            pltpu.VMEM((2, N, W), BF16),
            pltpu.VMEM((N, N, W), BF16),
            pltpu.VMEM((W, W), F32),
            pltpu.VMEM((W, W), F32),
            pltpu.VMEM((N, N, W), BF16),
            pltpu.VMEM((N, N, W), BF16),
            pltpu.VMEM((N, N, W), BF16),
            pltpu.VMEM((N, W), BF16),
            pltpu.VMEM((N, W), BF16),
            pltpu.VMEM((N, 2, N, W), BF16),
            pltpu.VMEM((N, 1, W), jnp.int32),
            pltpu.VMEM((N, 2, N, W), BF16),
            pltpu.VMEM((2, W, 2 * W), F32),
            dma(INPUTS),
            dma(3, N),
            dma(3, N),
            dma(N),
            dma(N),
            dma(n_batch // 2),
            dma(n_batch // 2),
            pltpu.SemaphoreType.DMA,
            pltpu.SemaphoreType.DMA,
            pltpu.SemaphoreType.DMA,
            pltpu.SemaphoreType.DMA,
            pltpu.SemaphoreType.DMA,
            pltpu.SemaphoreType.DMA,
            dma(N),
            dma(N),
        ],
        compiler_params=pltpu.CompilerParams(
            collective_id=0, has_side_effects=True, vmem_limit_bytes=63 * 1024 * 1024
        ),
    )(*inputs)
    gated = (gate * second.reshape(W, W).astype(F32)).astype(BF16)
    return dot(gated, out_proj, ((0,), (0,))).astype(BF16)


def solution(mesh):
    return jax.shard_map(
        functools.partial(body, mesh.shape["batch"]),
        mesh=mesh,
        in_specs=(
            P(("batch", "seq"), None),
            P(("batch", "seq")),
            P("batch"),
            P("seq", None, None),
            P(),
            P(),
            P(),
            P(),
        ),
        out_specs=P(("batch", "seq"), None),
        check_vma=False,
    )
```

```python
import functools
import math

import jax
import jax.numpy as jnp
import ml_dtypes
import numpy as np
from jax import lax
from jax.experimental import pallas as pl
from jax.experimental.pallas import tpu as pltpu
from jax.sharding import PartitionSpec as P

N = 16
FAR = (8, 7, 9, 6, 10, 5, 11, 4, 12, 3, 13, 2, 14, 1, 15)
W = 256
POINTS = 2 * N * W
F32, BF16 = jnp.float32, jnp.bfloat16


def split(table):
    high = table.astype(ml_dtypes.bfloat16)
    low = (table - high.astype(np.float64)).astype(ml_dtypes.bfloat16)
    return high, low


@functools.cache
def make_tables():
    half = np.arange(N) + 0.5
    outer = 2 * np.pi * np.outer(half, np.arange(N)) / (2 * N)
    eye = np.eye(N)
    fwd_a = np.concatenate([np.kron(np.cos(outer), eye), np.kron(-np.sin(outer), eye)], 0)
    inv_a = np.concatenate([np.kron(np.cos(outer.T), eye), np.kron(-np.sin(outer.T), eye)], 1) * (2.0 / POINTS)
    inner = 2 * np.pi * (np.outer(np.arange(W), np.arange(W)) % W) / W
    cos, sin = np.cos(inner), np.sin(inner)
    fwd_b = np.block([[cos, -sin], [sin, cos]])
    inv_b = np.block([[cos, sin], [-sin, cos]])
    twist = 2 * np.pi * np.outer(half, np.arange(W)) / POINTS
    cat = lambda table, axis, order=(0, 0, 1): np.concatenate([split(table)[i] for i in order], axis)
    return (
        cat(fwd_a, 1),
        cat(fwd_b, 0, (0, 1)),
        cat(inv_b, 0, (0, 1)),
        cat(inv_a, 1),
        np.stack([np.cos(twist), np.sin(twist)]).astype(np.float32),
    )


def parts(x, axis):
    high = x.astype(BF16)
    low = (x - high.astype(F32)).astype(BF16)
    return jnp.concatenate([high, low, high], axis=axis)


def dot(a, b, dims=((1,), (0,))):
    return lax.dot_general(a, b, (dims, ((), ())), preferred_element_type=F32)


INPUTS = 12


def kernel(n_batch, *refs):
    outside, (out, side, *inside), rest = refs[:INPUTS], refs[INPUTS : 2 * INPUTS + 2], refs[2 * INPUTS + 2 :]
    length, positions, events, filters, skip_gain, short_filter, in_proj, *tables = inside
    fwd_a, fwd_b, inv_b, inv_a, twist = tables
    (
        thirds,
        block_row,
        taps,
        gated,
        gate,
        passed,
        ids_row,
        sent_rows,
        recv_rows,
        tail_rows,
        halo,
        recv_sig,
        recv_blk,
        recv_tap,
        spec,
        load_sem,
        sig_send,
        sig_recv,
        blk_send,
        blk_recv,
        tap_send,
        tap_recv,
        own_send,
        own_recv,
        keep_sem,
        side_sem,
        halo_send,
        halo_recv,
        out_send,
        out_recv,
    ) = rest
    me = lax.axis_index("seq")
    lane = lax.axis_index("batch")
    column, core = lane // 2, lane % 2
    chips = n_batch // 2
    side_len = math.isqrt(chips)
    plane = [(dy, dx) for dy in range(side_len) for dx in range(side_len) if dy or dx]
    shift = (column + N // 2 * core) % N
    target = (me + shift) % N

    barrier = pltpu.get_barrier_semaphore()

    def chip_at(dy, dx):
        return (column // side_len + dy) % side_len * side_len + (column + dx) % side_len

    hops = [(min(k, N - k), k) for k in FAR]
    hops += [(min(dy, side_len - dy) + min(dx, side_len - dx), (dy, dx)) for dy, dx in plane]
    hops.sort(key=lambda item: -item[0])

    def greet(some):
        for _, to in some:
            if isinstance(to, tuple):
                peer = {"batch": chip_at(*to) * 2 + core}
            else:
                peer = {"seq": (me + to) % N}
            pl.semaphore_signal(barrier, inc=1, device_id=peer)

    greet(hops[: len(hops) // 2])
    loads = []
    for i, (src, dst) in enumerate(zip(outside, inside)):
        if i == 3:
            src = src.at[:, :, pl.ds(pl.multiple_of(target // 8 * 128, 128), 128)]
        loads.append(pltpu.make_async_copy(src, dst, load_sem.at[i]))
    for i in (1, 2, 6, 0, 3):
        loads[i].start()
    greet(hops[len(hops) // 2 :])
    for i in (7, 11, 8, 5, 4, 9, 10):
        loads[i].start()

    for i in (1, 0, 2, 6):
        loads[i].wait()
    pos = positions[...]
    order = lax.broadcasted_iota(jnp.int32, (W, W), 0) == pos % W
    one_hot = order.astype(BF16)
    kept = jnp.where(pos < length[...], one_hot, jnp.zeros_like(one_hot))
    ids = jnp.broadcast_to((pos // W).astype(BF16), (N, W))
    block_row[...] = dot(ids, one_hot, ((1,), (1,)))[0:1].astype(jnp.int32)
    ordered = dot(kept, events[...]).astype(BF16)

    def project(t):
        projected = dot(ordered, in_proj[:, t * W : (t + 1) * W])
        thirds[:, t] = projected.T.astype(BF16).reshape(N, N, W)

    project(0)
    loads[3].wait()
    rows16 = lax.broadcasted_iota(jnp.int32, (N, W), 0)
    lanes16 = lax.broadcasted_iota(jnp.int32, (N, W), 1)
    pick = (lanes16[:, :128] == rows16[:, :128] + target % 8 * N).astype(BF16)
    for f in range(2):
        taps[f] = dot(pick, filters[:, f, :].astype(BF16), ((1,), (1,))).astype(BF16)
    pl.semaphore_wait(barrier, N - 1 + chips - 1)

    def tap_first():
        return pltpu.make_async_remote_copy(
            src_ref=taps,
            dst_ref=recv_tap.at[me],
            send_sem=own_send,
            recv_sem=own_recv,
            device_id={"seq": target},
        )

    slot = (me + N - shift) % N

    def block_copy(k):
        peer = (me + k) % N
        return pltpu.make_async_remote_copy(
            src_ref=block_row,
            dst_ref=recv_blk.at[me],
            send_sem=blk_send.at[peer],
            recv_sem=blk_recv.at[me],
            device_id={"seq": peer},
        )

    def block_arrival(k):
        peer = (me + k) % N
        return pltpu.make_async_remote_copy(
            src_ref=block_row,
            dst_ref=recv_blk.at[peer],
            send_sem=blk_send.at[peer],
            recv_sem=blk_recv.at[peer],
            device_id={"seq": peer},
        )

    def third_copy(part, k):
        peer = (me + k) % N
        return pltpu.make_async_remote_copy(
            src_ref=thirds.at[peer, part],
            dst_ref=recv_sig.at[me, part],
            send_sem=sig_send.at[part, peer],
            recv_sem=sig_recv.at[part, me],
            device_id={"seq": peer},
        )

    def third_arrival(part, k):
        peer = (me + k) % N
        return pltpu.make_async_remote_copy(
            src_ref=thirds.at[peer, part],
            dst_ref=recv_sig.at[peer, part],
            send_sem=sig_send.at[part, peer],
            recv_sem=sig_recv.at[part, peer],
            device_id={"seq": peer},
        )

    def each(count, act):
        def step(k, carry):
            act(k)
            return carry

        lax.fori_loop(1, count, step, 0)

    @pl.when(shift != 0)
    def _():
        tap_first().start()

    @pl.when(shift == 0)
    def _():
        recv_tap[me] = taps[...]

    for k in FAR:
        block_copy(k).start()
        third_copy(0, k).start()
    project(1)
    for k in FAR:
        third_copy(1, k).start()
    by_block = lax.broadcasted_iota(jnp.int32, (W, W), 0) == pos // W * N + pos % N
    by_block = jnp.where(by_block & (pos < length[...]), 1.0, 0.0).astype(BF16)
    rows = dot(by_block, events[...]).astype(BF16)
    sent_rows[...] = dot(rows, in_proj[:, 2 * W :]).astype(BF16).reshape(N, N, W)
    recv_rows[me] = sent_rows[me]
    recv_blk[me] = block_row[...]
    recv_sig[me] = thirds[me]

    def rows_copy(k):
        peer = (me + k) % N
        return pltpu.make_async_remote_copy(
            src_ref=sent_rows.at[peer],
            dst_ref=recv_rows.at[me],
            send_sem=sig_send.at[2, peer],
            recv_sem=sig_recv.at[2, me],
            device_id={"seq": peer},
        )

    def rows_arrival(k):
        peer = (me + k) % N
        return pltpu.make_async_remote_copy(
            src_ref=sent_rows.at[peer],
            dst_ref=recv_rows.at[peer],
            send_sem=sig_send.at[2, peer],
            recv_sem=sig_recv.at[2, peer],
            device_id={"seq": peer},
        )

    def halo_copy(step):
        return pltpu.make_async_remote_copy(
            src_ref=tail_rows,
            dst_ref=halo,
            send_sem=halo_send,
            recv_sem=halo_recv,
            device_id={"seq": (me + step) % N},
        )

    for k in FAR:
        rows_copy(k).start()

    @pl.when(shift != 0)
    def _():
        pltpu.make_async_remote_copy(
            src_ref=taps,
            dst_ref=recv_tap.at[slot],
            send_sem=own_send,
            recv_sem=own_recv,
            device_id={"seq": target},
        ).wait_recv()

    def tap_copy(peer):
        return pltpu.make_async_remote_copy(
            src_ref=recv_tap.at[slot],
            dst_ref=recv_tap.at[slot],
            send_sem=tap_send.at[peer],
            recv_sem=tap_recv.at[column],
            device_id={"batch": peer * 2 + core},
        )

    def tap_arrival(k):
        peer = (column + k) % chips
        there = recv_tap.at[(me + N - (peer + N // 2 * core) % N) % N]
        return pltpu.make_async_remote_copy(
            src_ref=there,
            dst_ref=there,
            send_sem=tap_send.at[peer],
            recv_sem=tap_recv.at[peer],
            device_id={"batch": peer * 2 + core},
        )

    for _, to in hops:
        if isinstance(to, tuple):
            tap_copy(chip_at(*to)).start()

    def column_of(row):
        return jnp.sum(jnp.where(lanes16 == rows16 + me * N, row, 0.0), axis=1, keepdims=True)[None]

    def rotate(re, im, sign):
        cos = twist[0][:, None, :]
        sin = twist[1][:, None, :] * sign
        re, im = re.reshape(N, N, W), im.reshape(N, N, W)
        return (re * cos + im * sin).reshape(W, W), (im * cos - re * sin).reshape(W, W)

    def inner(re, im, table):
        x = jnp.concatenate([re, im], axis=1).astype(BF16)
        return dot(jnp.concatenate([x, x], axis=1), table[...])

    def forward(signal):
        if signal.dtype == BF16:
            mid = dot(fwd_a[:, W:], jnp.concatenate([signal, signal], axis=0))
        else:
            mid = dot(fwd_a[...], parts(signal, 0))
        re, im = rotate(mid[:W], mid[W:], 1.0)
        return inner(re, im, fwd_b)

    def filtered(got, f):
        re, im = got[:, :W], got[:, W:]
        tap_re, tap_im = spec[f, :, :W], spec[f, :, W:]
        re, im = re * tap_re - im * tap_im, re * tap_im + im * tap_re
        mid = inner(re, im, inv_b)
        re, im = rotate(mid[:, :W], mid[:, W:], -1.0)
        return parts(jnp.concatenate([re, im], axis=0), 0)

    sub = lax.broadcasted_iota(jnp.int32, (W, W), 1)

    def short(t):
        rows = []
        for b in range(N):
            total = jnp.zeros((N, W), BF16)
            for s in range(N):
                total = jnp.where(ids_row[s] == b, recv_sig[s, t], total)
            rows.append(total)
        stream = jnp.concatenate(rows, axis=0).astype(F32)
        before = jnp.concatenate([jnp.zeros((N, W), F32), stream[:-N]], axis=0)
        one = pltpu.roll(jnp.where(sub == W - 1, before, stream), 1, 1)
        two = pltpu.roll(jnp.where(sub >= W - 2, before, stream), 2, 1)
        tap = [column_of(short_filter[i : i + 1, t * W : (t + 1) * W]) for i in range(3)]
        blocks = lambda x: x.reshape(N, N, W)
        return (tap[0] * blocks(stream) + tap[1] * blocks(one) + tap[2] * blocks(two)).reshape(W, W)

    for i in (7, 11, 8, 5, 4, 9, 10):
        loads[i].wait()
    gain = [column_of(skip_gain[i : i + 1, :]) for i in range(2)]
    scaled = lambda g, x: (g * x.reshape(-1, N, W)).reshape(-1, W)
    spectrum = lambda f: forward(recv_tap[:, f].reshape(W, W))

    for k in FAR[::-1]:
        block_arrival(k).wait_recv()
    for s in range(N):
        ids_row[s] = jnp.broadcast_to(recv_blk[s].astype(F32), (N, W)).astype(BF16)
    for k in FAR[::-1]:
        third_arrival(0, k).wait_recv()
    value = short(0)
    ahead = forward(value)
    for k in FAR[::-1]:
        third_arrival(1, k).wait_recv()
    gate[...] = short(1)
    for k in range(1, chips):
        tap_arrival(k).wait_recv()
    spec[0] = spectrum(0)
    first = gate[...] * (dot(inv_a[...], filtered(ahead, 0)) + scaled(gain[0], value))
    passed[...] = scaled(gain[1], first)
    spec[1] = spectrum(1)
    ahead = filtered(forward(first), 1)
    def out_copy(k):
        peer = (me + k) % N
        return pltpu.make_async_remote_copy(
            src_ref=gated.at[peer],
            dst_ref=out.at[me],
            send_sem=out_send.at[peer],
            recv_sem=out_recv.at[me],
            device_id={"seq": peer},
        )

    def out_arrival(k):
        peer = (me + k) % N
        return pltpu.make_async_remote_copy(
            src_ref=gated.at[peer],
            dst_ref=out.at[peer],
            send_sem=out_send.at[peer],
            recv_sem=out_recv.at[peer],
            device_id={"seq": peer},
        )

    gated[...] = (dot(inv_a[...], ahead) + passed[...]).astype(BF16).reshape(N, N, W)
    for k in FAR:
        out_copy(k).start()
    own = pltpu.make_async_copy(gated.at[me], out.at[me], keep_sem)
    own.start()

    up = lax.broadcasted_iota(jnp.int32, (W, W), 0)
    place = (ids_row[...].reshape(W, W).astype(F32) == me.astype(F32)) & (up % N == sub % N)
    for k in FAR[::-1]:
        rows_arrival(k).wait_recv()
    stream = dot(jnp.where(place, 1.0, 0.0).astype(BF16), recv_rows[...].reshape(W, W), ((0,), (0,)))
    tail_rows[...] = stream[W - N :].astype(BF16)

    @pl.when(me < N - 1)
    def _():
        halo_copy(1).start()

    tap = [short_filter[i : i + 1, 2 * W :] for i in range(3)]
    one = jnp.where(up == 0, 0.0, pltpu.roll(stream, 1, 0))
    two = jnp.where(up <= 1, 0.0, pltpu.roll(stream, 2, 0))
    gate[...] = (tap[0] * stream + tap[1] * one + tap[2] * two).T
    halves = [
        pltpu.make_async_copy(gate.at[:, pl.ds(i * 128, 128)], side.at[:, pl.ds(i * 128, 128)], side_sem.at[i])
        for i in range(2)
    ]
    halves[1].start()

    @pl.when(me == 0)
    def _():
        halo[...] = jnp.zeros_like(halo)

    @pl.when(me > 0)
    def _():
        halo_copy(N - 1).wait_recv()

    edge = halo[...].astype(F32)
    last, ahead_of = edge[N - 1 :], edge[N - 2 : N - 1]
    first_rows = jnp.where(up == 0, tap[1] * last + tap[2] * ahead_of, jnp.where(up == 1, tap[2] * last, 0.0))[:128]
    gate[:, :128] += first_rows.T
    halves[0].start()

    @pl.when(shift != 0)
    def _():
        tap_first().wait_send()

    each(N, lambda k: block_copy(k).wait_send())
    for part in range(2):
        each(N, lambda k: third_copy(part, k).wait_send())
    each(N, lambda k: rows_copy(k).wait_send())

    @pl.when(me < N - 1)
    def _():
        halo_copy(1).wait_send()

    each(chips, lambda k: tap_copy((column + k) % chips).wait_send())
    each(N, lambda k: out_copy(k).wait_send())
    for k in FAR[::-1]:
        out_arrival(k).wait_recv()
    own.wait()
    for half in halves:
        half.wait()


def body(n_batch, events, positions, length, filters, skip_gain, short_filter, in_proj, out_proj):
    tables = [jnp.asarray(table) for table in make_tables()]
    inputs = [
        length.reshape(1, 1),
        positions.reshape(1, W),
        events,
        filters,
        skip_gain,
        short_filter,
        in_proj,
        *tables,
    ]
    dma = lambda *shape: pltpu.SemaphoreType.DMA(shape)
    held = [pltpu.VMEM((W, 2, 128) if i == 3 else x.shape, x.dtype) for i, x in enumerate(inputs)]
    second, gate = pl.pallas_call(
        functools.partial(kernel, n_batch),
        out_shape=(jax.ShapeDtypeStruct((N, N, W), BF16), jax.ShapeDtypeStruct((W, W), F32)),
        in_specs=[pl.BlockSpec(memory_space=pl.ANY)] * INPUTS,
        out_specs=(pl.BlockSpec(memory_space=pl.ANY),) * 2,
        scratch_shapes=held
        + [
            pltpu.VMEM((N, 2, N, W), BF16),
            pltpu.VMEM((1, W), jnp.int32),
            pltpu.VMEM((2, N, W), BF16),
            pltpu.VMEM((N, N, W), BF16),
            pltpu.VMEM((W, W), F32),
            pltpu.VMEM((W, W), F32),
            pltpu.VMEM((N, N, W), BF16),
            pltpu.VMEM((N, N, W), BF16),
            pltpu.VMEM((N, N, W), BF16),
            pltpu.VMEM((N, W), BF16),
            pltpu.VMEM((N, W), BF16),
            pltpu.VMEM((N, 2, N, W), BF16),
            pltpu.VMEM((N, 1, W), jnp.int32),
            pltpu.VMEM((N, 2, N, W), BF16),
            pltpu.VMEM((2, W, 2 * W), F32),
            dma(INPUTS),
            dma(3, N),
            dma(3, N),
            dma(N),
            dma(N),
            dma(n_batch // 2),
            dma(n_batch // 2),
            pltpu.SemaphoreType.DMA,
            pltpu.SemaphoreType.DMA,
            pltpu.SemaphoreType.DMA,
            dma(2),
            pltpu.SemaphoreType.DMA,
            pltpu.SemaphoreType.DMA,
            dma(N),
            dma(N),
        ],
        compiler_params=pltpu.CompilerParams(
            collective_id=0, has_side_effects=True, vmem_limit_bytes=63 * 1024 * 1024
        ),
    )(*inputs)
    gated = (gate * second.reshape(W, W).astype(F32)).astype(BF16)
    return dot(gated, out_proj, ((0,), (0,))).astype(BF16)


def solution(mesh):
    return jax.shard_map(
        functools.partial(body, mesh.shape["batch"]),
        mesh=mesh,
        in_specs=(
            P(("batch", "seq"), None),
            P(("batch", "seq")),
            P("batch"),
            P("seq", None, None),
            P(),
            P(),
            P(),
            P(),
        ),
        out_specs=P(("batch", "seq"), None),
        check_vma=False,
    )
```

```python
import functools
import math

import jax
import jax.numpy as jnp
import ml_dtypes
import numpy as np
from jax import lax
from jax.experimental import pallas as pl
from jax.experimental.pallas import tpu as pltpu
from jax.sharding import PartitionSpec as P

N = 16
FAR = (8, 7, 9, 6, 10, 5, 11, 4, 12, 3, 13, 2, 14, 1, 15)
W = 256
POINTS = 2 * N * W
F32, BF16 = jnp.float32, jnp.bfloat16


def split(table):
    high = table.astype(ml_dtypes.bfloat16)
    low = (table - high.astype(np.float64)).astype(ml_dtypes.bfloat16)
    return high, low


@functools.cache
def make_tables():
    half = np.arange(N) + 0.5
    outer = 2 * np.pi * np.outer(half, np.arange(N)) / (2 * N)
    eye = np.eye(N)
    fwd_a = np.concatenate([np.kron(np.cos(outer), eye), np.kron(-np.sin(outer), eye)], 0)
    inv_a = np.concatenate([np.kron(np.cos(outer.T), eye), np.kron(-np.sin(outer.T), eye)], 1) * (2.0 / POINTS)
    inner = 2 * np.pi * (np.outer(np.arange(W), np.arange(W)) % W) / W
    cos, sin = np.cos(inner), np.sin(inner)
    fwd_b = np.block([[cos, -sin], [sin, cos]])
    inv_b = np.block([[cos, sin], [-sin, cos]])
    twist = 2 * np.pi * np.outer(half, np.arange(W)) / POINTS
    cat = lambda table, axis, order=(0, 0, 1): np.concatenate([split(table)[i] for i in order], axis)
    return (
        cat(fwd_a, 1),
        cat(fwd_b, 0, (0, 1)),
        cat(inv_b, 0, (0, 1)),
        cat(inv_a, 1),
        np.stack([np.cos(twist), np.sin(twist)]).astype(np.float32),
    )


def parts(x, axis):
    high = x.astype(BF16)
    low = (x - high.astype(F32)).astype(BF16)
    return jnp.concatenate([high, low, high], axis=axis)


def dot(a, b, dims=((1,), (0,))):
    return lax.dot_general(a, b, (dims, ((), ())), preferred_element_type=F32)


INPUTS = 12


def kernel(n_batch, *refs):
    outside, (out, side, *inside), rest = refs[:INPUTS], refs[INPUTS : 2 * INPUTS + 2], refs[2 * INPUTS + 2 :]
    length, positions, events, filters, skip_gain, short_filter, in_proj, *tables = inside
    fwd_a, fwd_b, inv_b, inv_a, twist = tables
    (
        thirds,
        block_row,
        taps,
        gated,
        gate,
        passed,
        ids_row,
        sent_rows,
        recv_rows,
        tail_rows,
        halo,
        recv_sig,
        recv_blk,
        recv_tap,
        spec,
        load_sem,
        sig_send,
        sig_recv,
        blk_send,
        blk_recv,
        tap_send,
        tap_recv,
        own_send,
        own_recv,
        keep_sem,
        side_sem,
        halo_send,
        halo_recv,
        out_send,
        out_recv,
    ) = rest
    me = lax.axis_index("seq")
    lane = lax.axis_index("batch")
    column, core = lane // 2, lane % 2
    chips = n_batch // 2
    side_len = math.isqrt(chips)
    plane = [(dy, dx) for dy in range(side_len) for dx in range(side_len) if dy or dx]
    shift = (column + N // 2 * core) % N
    target = (me + shift) % N

    barrier = pltpu.get_barrier_semaphore()

    def chip_at(dy, dx):
        return (column // side_len + dy) % side_len * side_len + (column + dx) % side_len

    hops = [(min(k, N - k), k) for k in FAR]
    hops += [(min(dy, side_len - dy) + min(dx, side_len - dx), (dy, dx)) for dy, dx in plane]
    hops.sort(key=lambda item: -item[0])

    def greet(some):
        for _, to in some:
            if isinstance(to, tuple):
                peer = {"batch": chip_at(*to) * 2 + core}
            else:
                peer = {"seq": (me + to) % N}
            pl.semaphore_signal(barrier, inc=1, device_id=peer)

    greet(hops[: len(hops) // 2])
    loads = []
    for i, (src, dst) in enumerate(zip(outside, inside)):
        if i == 3:
            src = src.at[:, :, pl.ds(pl.multiple_of(target // 8 * 128, 128), 128)]
        loads.append(pltpu.make_async_copy(src, dst, load_sem.at[i]))
    for i in (1, 2, 6, 0, 3):
        loads[i].start()
    greet(hops[len(hops) // 2 :])
    for i in (7, 11, 8, 5, 4, 9, 10):
        loads[i].start()

    for i in (1, 0, 2, 6):
        loads[i].wait()
    pos = positions[...]
    order = lax.broadcasted_iota(jnp.int32, (W, W), 0) == pos % W
    one_hot = order.astype(BF16)
    kept = jnp.where(pos < length[...], one_hot, jnp.zeros_like(one_hot))
    ids = jnp.broadcast_to((pos // W).astype(BF16), (N, W))
    block_row[...] = dot(ids, one_hot, ((1,), (1,)))[0:1].astype(jnp.int32)
    ordered = dot(kept, events[...]).astype(BF16)

    def project(t):
        projected = dot(ordered, in_proj[:, t * W : (t + 1) * W])
        thirds[:, t] = projected.T.astype(BF16).reshape(N, N, W)

    project(0)
    loads[3].wait()
    rows16 = lax.broadcasted_iota(jnp.int32, (N, W), 0)
    lanes16 = lax.broadcasted_iota(jnp.int32, (N, W), 1)
    pick = (lanes16[:, :128] == rows16[:, :128] + target % 8 * N).astype(BF16)
    for f in range(2):
        taps[f] = dot(pick, filters[:, f, :].astype(BF16), ((1,), (1,))).astype(BF16)
    pl.semaphore_wait(barrier, N - 1 + chips - 1)

    def tap_first():
        return pltpu.make_async_remote_copy(
            src_ref=taps,
            dst_ref=recv_tap.at[me],
            send_sem=own_send,
            recv_sem=own_recv,
            device_id={"seq": target},
        )

    slot = (me + N - shift) % N

    def block_copy(k):
        peer = (me + k) % N
        return pltpu.make_async_remote_copy(
            src_ref=block_row,
            dst_ref=recv_blk.at[me],
            send_sem=blk_send.at[peer],
            recv_sem=blk_recv.at[me],
            device_id={"seq": peer},
        )

    def block_arrival(k):
        peer = (me + k) % N
        return pltpu.make_async_remote_copy(
            src_ref=block_row,
            dst_ref=recv_blk.at[peer],
            send_sem=blk_send.at[peer],
            recv_sem=blk_recv.at[peer],
            device_id={"seq": peer},
        )

    def third_copy(part, k):
        peer = (me + k) % N
        return pltpu.make_async_remote_copy(
            src_ref=thirds.at[peer, part],
            dst_ref=recv_sig.at[me, part],
            send_sem=sig_send.at[part, peer],
            recv_sem=sig_recv.at[part, me],
            device_id={"seq": peer},
        )

    def third_arrival(part, k):
        peer = (me + k) % N
        return pltpu.make_async_remote_copy(
            src_ref=thirds.at[peer, part],
            dst_ref=recv_sig.at[peer, part],
            send_sem=sig_send.at[part, peer],
            recv_sem=sig_recv.at[part, peer],
            device_id={"seq": peer},
        )

    def each(count, act):
        def step(k, carry):
            act(k)
            return carry

        lax.fori_loop(1, count, step, 0)

    @pl.when(shift != 0)
    def _():
        tap_first().start()

    @pl.when(shift == 0)
    def _():
        recv_tap[me] = taps[...]

    for k in FAR:
        block_copy(k).start()
        third_copy(0, k).start()
    project(1)
    for k in FAR:
        third_copy(1, k).start()
    by_block = lax.broadcasted_iota(jnp.int32, (W, W), 0) == pos // W * N + pos % N
    by_block = jnp.where(by_block & (pos < length[...]), 1.0, 0.0).astype(BF16)
    rows = dot(by_block, events[...]).astype(BF16)
    sent_rows[...] = dot(rows, in_proj[:, 2 * W :]).astype(BF16).reshape(N, N, W)
    recv_rows[me] = sent_rows[me]
    recv_blk[me] = block_row[...]
    recv_sig[me] = thirds[me]

    def rows_copy(k):
        peer = (me + k) % N
        return pltpu.make_async_remote_copy(
            src_ref=sent_rows.at[peer],
            dst_ref=recv_rows.at[me],
            send_sem=sig_send.at[2, peer],
            recv_sem=sig_recv.at[2, me],
            device_id={"seq": peer},
        )

    def rows_arrival(k):
        peer = (me + k) % N
        return pltpu.make_async_remote_copy(
            src_ref=sent_rows.at[peer],
            dst_ref=recv_rows.at[peer],
            send_sem=sig_send.at[2, peer],
            recv_sem=sig_recv.at[2, peer],
            device_id={"seq": peer},
        )

    def halo_copy(step):
        return pltpu.make_async_remote_copy(
            src_ref=tail_rows,
            dst_ref=halo,
            send_sem=halo_send,
            recv_sem=halo_recv,
            device_id={"seq": (me + step) % N},
        )

    @pl.when(shift != 0)
    def _():
        pltpu.make_async_remote_copy(
            src_ref=taps,
            dst_ref=recv_tap.at[slot],
            send_sem=own_send,
            recv_sem=own_recv,
            device_id={"seq": target},
        ).wait_recv()

    def tap_copy(peer):
        return pltpu.make_async_remote_copy(
            src_ref=recv_tap.at[slot],
            dst_ref=recv_tap.at[slot],
            send_sem=tap_send.at[peer],
            recv_sem=tap_recv.at[column],
            device_id={"batch": peer * 2 + core},
        )

    def tap_arrival(k):
        peer = (column + k) % chips
        there = recv_tap.at[(me + N - (peer + N // 2 * core) % N) % N]
        return pltpu.make_async_remote_copy(
            src_ref=there,
            dst_ref=there,
            send_sem=tap_send.at[peer],
            recv_sem=tap_recv.at[peer],
            device_id={"batch": peer * 2 + core},
        )

    for _, to in hops:
        if isinstance(to, tuple):
            tap_copy(chip_at(*to)).start()
    for k in FAR:
        rows_copy(k).start()

    def column_of(row):
        return jnp.sum(jnp.where(lanes16 == rows16 + me * N, row, 0.0), axis=1, keepdims=True)[None]

    def rotate(re, im, sign):
        cos = twist[0][:, None, :]
        sin = twist[1][:, None, :] * sign
        re, im = re.reshape(N, N, W), im.reshape(N, N, W)
        return (re * cos + im * sin).reshape(W, W), (im * cos - re * sin).reshape(W, W)

    def inner(re, im, table):
        x = jnp.concatenate([re, im], axis=1).astype(BF16)
        return dot(jnp.concatenate([x, x], axis=1), table[...])

    def forward(signal):
        mid = dot(fwd_a[...], parts(signal, 0))
        return inner(*rotate(mid[:W], mid[W:], 1.0), fwd_b)

    def spectra():
        sides = []
        for f in range(2):
            lags = recv_tap[:, f].reshape(W, W)
            mid = dot(fwd_a[:, W:], jnp.concatenate([lags, lags], axis=0))
            sides.append(rotate(mid[:W], mid[W:], 1.0))
        spec[...] = inner(*(jnp.concatenate(x, axis=0) for x in zip(*sides)), fwd_b).reshape(2, W, 2 * W)

    def filtered(got, f):
        re, im = got[:, :W], got[:, W:]
        tap_re, tap_im = spec[f, :, :W], spec[f, :, W:]
        re, im = re * tap_re - im * tap_im, re * tap_im + im * tap_re
        mid = inner(re, im, inv_b)
        re, im = rotate(mid[:, :W], mid[:, W:], -1.0)
        return parts(jnp.concatenate([re, im], axis=0), 0)

    sub = lax.broadcasted_iota(jnp.int32, (W, W), 1)

    def short(t):
        rows = []
        for b in range(N):
            total = jnp.zeros((N, W), BF16)
            for s in range(N):
                total = jnp.where(ids_row[s] == b, recv_sig[s, t], total)
            rows.append(total)
        stream = jnp.concatenate(rows, axis=0).astype(F32)
        before = jnp.concatenate([jnp.zeros((N, W), F32), stream[:-N]], axis=0)
        one = pltpu.roll(jnp.where(sub == W - 1, before, stream), 1, 1)
        two = pltpu.roll(jnp.where(sub >= W - 2, before, stream), 2, 1)
        tap = [column_of(short_filter[i : i + 1, t * W : (t + 1) * W]) for i in range(3)]
        blocks = lambda x: x.reshape(N, N, W)
        return (tap[0] * blocks(stream) + tap[1] * blocks(one) + tap[2] * blocks(two)).reshape(W, W)

    for i in (7, 11, 8, 5, 4, 9, 10):
        loads[i].wait()
    gain = [column_of(skip_gain[i : i + 1, :]) for i in range(2)]
    scaled = lambda g, x: (g * x.reshape(-1, N, W)).reshape(-1, W)

    for k in FAR[::-1]:
        block_arrival(k).wait_recv()
    for s in range(N):
        ids_row[s] = jnp.broadcast_to(recv_blk[s].astype(F32), (N, W)).astype(BF16)
    for k in FAR[::-1]:
        third_arrival(0, k).wait_recv()
    value = short(0)
    ahead = forward(value)
    for k in FAR[::-1]:
        third_arrival(1, k).wait_recv()
    gate[...] = short(1)
    for k in range(1, chips):
        tap_arrival(k).wait_recv()
    spectra()
    first = gate[...] * (dot(inv_a[...], filtered(ahead, 0)) + scaled(gain[0], value))
    passed[...] = scaled(gain[1], first)
    ahead = filtered(forward(first), 1)
    def out_copy(k):
        peer = (me + k) % N
        return pltpu.make_async_remote_copy(
            src_ref=gated.at[peer],
            dst_ref=out.at[me],
            send_sem=out_send.at[peer],
            recv_sem=out_recv.at[me],
            device_id={"seq": peer},
        )

    def out_arrival(k):
        peer = (me + k) % N
        return pltpu.make_async_remote_copy(
            src_ref=gated.at[peer],
            dst_ref=out.at[peer],
            send_sem=out_send.at[peer],
            recv_sem=out_recv.at[peer],
            device_id={"seq": peer},
        )

    gated[...] = (dot(inv_a[...], ahead) + passed[...]).astype(BF16).reshape(N, N, W)
    for k in FAR:
        out_copy(k).start()
    own = pltpu.make_async_copy(gated.at[me], out.at[me], keep_sem)
    own.start()

    up = lax.broadcasted_iota(jnp.int32, (W, W), 0)
    place = (ids_row[...].reshape(W, W).astype(F32) == me.astype(F32)) & (up % N == sub % N)
    for k in FAR[::-1]:
        rows_arrival(k).wait_recv()
    stream = dot(jnp.where(place, 1.0, 0.0).astype(BF16), recv_rows[...].reshape(W, W), ((0,), (0,)))
    tail_rows[...] = stream[W - N :].astype(BF16)

    @pl.when(me < N - 1)
    def _():
        halo_copy(1).start()

    tap = [short_filter[i : i + 1, 2 * W :] for i in range(3)]
    one = jnp.where(up == 0, 0.0, pltpu.roll(stream, 1, 0))
    two = jnp.where(up <= 1, 0.0, pltpu.roll(stream, 2, 0))
    gate[...] = (tap[0] * stream + tap[1] * one + tap[2] * two).T
    halves = [
        pltpu.make_async_copy(gate.at[:, pl.ds(i * 128, 128)], side.at[:, pl.ds(i * 128, 128)], side_sem.at[i])
        for i in range(2)
    ]
    halves[1].start()

    @pl.when(me == 0)
    def _():
        halo[...] = jnp.zeros_like(halo)

    @pl.when(me > 0)
    def _():
        halo_copy(N - 1).wait_recv()

    edge = halo[...].astype(F32)
    last, ahead_of = edge[N - 1 :], edge[N - 2 : N - 1]
    first_rows = jnp.where(up == 0, tap[1] * last + tap[2] * ahead_of, jnp.where(up == 1, tap[2] * last, 0.0))[:128]
    gate[:, :128] += first_rows.T
    halves[0].start()

    @pl.when(shift != 0)
    def _():
        tap_first().wait_send()

    each(N, lambda k: block_copy(k).wait_send())
    for part in range(2):
        each(N, lambda k: third_copy(part, k).wait_send())
    each(N, lambda k: rows_copy(k).wait_send())

    @pl.when(me < N - 1)
    def _():
        halo_copy(1).wait_send()

    each(chips, lambda k: tap_copy((column + k) % chips).wait_send())
    each(N, lambda k: out_copy(k).wait_send())
    for k in FAR[::-1]:
        out_arrival(k).wait_recv()
    own.wait()
    for half in halves:
        half.wait()


def body(n_batch, events, positions, length, filters, skip_gain, short_filter, in_proj, out_proj):
    tables = [jnp.asarray(table) for table in make_tables()]
    inputs = [
        length.reshape(1, 1),
        positions.reshape(1, W),
        events,
        filters,
        skip_gain,
        short_filter,
        in_proj,
        *tables,
    ]
    dma = lambda *shape: pltpu.SemaphoreType.DMA(shape)
    held = [pltpu.VMEM((W, 2, 128) if i == 3 else x.shape, x.dtype) for i, x in enumerate(inputs)]
    second, gate = pl.pallas_call(
        functools.partial(kernel, n_batch),
        out_shape=(jax.ShapeDtypeStruct((N, N, W), BF16), jax.ShapeDtypeStruct((W, W), F32)),
        in_specs=[pl.BlockSpec(memory_space=pl.ANY)] * INPUTS,
        out_specs=(pl.BlockSpec(memory_space=pl.ANY),) * 2,
        scratch_shapes=held
        + [
            pltpu.VMEM((N, 2, N, W), BF16),
            pltpu.VMEM((1, W), jnp.int32),
            pltpu.VMEM((2, N, W), BF16),
            pltpu.VMEM((N, N, W), BF16),
            pltpu.VMEM((W, W), F32),
            pltpu.VMEM((W, W), F32),
            pltpu.VMEM((N, N, W), BF16),
            pltpu.VMEM((N, N, W), BF16),
            pltpu.VMEM((N, N, W), BF16),
            pltpu.VMEM((N, W), BF16),
            pltpu.VMEM((N, W), BF16),
            pltpu.VMEM((N, 2, N, W), BF16),
            pltpu.VMEM((N, 1, W), jnp.int32),
            pltpu.VMEM((N, 2, N, W), BF16),
            pltpu.VMEM((2, W, 2 * W), F32),
            dma(INPUTS),
            dma(3, N),
            dma(3, N),
            dma(N),
            dma(N),
            dma(n_batch // 2),
            dma(n_batch // 2),
            pltpu.SemaphoreType.DMA,
            pltpu.SemaphoreType.DMA,
            pltpu.SemaphoreType.DMA,
            dma(2),
            pltpu.SemaphoreType.DMA,
            pltpu.SemaphoreType.DMA,
            dma(N),
            dma(N),
        ],
        compiler_params=pltpu.CompilerParams(
            collective_id=0, has_side_effects=True, vmem_limit_bytes=63 * 1024 * 1024
        ),
    )(*inputs)
    gated = (gate * second.reshape(W, W).astype(F32)).astype(BF16)
    return dot(gated, out_proj, ((0,), (0,))).astype(BF16)


def solution(mesh):
    return jax.shard_map(
        functools.partial(body, mesh.shape["batch"]),
        mesh=mesh,
        in_specs=(
            P(("batch", "seq"), None),
            P(("batch", "seq")),
            P("batch"),
            P("seq", None, None),
            P(),
            P(),
            P(),
            P(),
        ),
        out_specs=P(("batch", "seq"), None),
        check_vma=False,
    )
```
